128 devices in a mesh: frame: 8 (over x, y_hi), pair: 16 (over y_lo, z, core).
Axes of the slice: x: 4, y: 4 (y_hi: 2, y_lo: 2; y = y_hi * 2 + y_lo), z: 4, core: 2. Of those that a mesh axis runs over, the one named last changes fastest.
Arguments:
- columns: float32 [16384, 16384], P('frame', 'pair')
- rotations: float32 [2, 32, 512, 512], P(None, 'pair'), as said below
- plan: int32 [2, 16, 4], P(None, 'pair'), may hold values from 0 to 3, as said below
Outputs:
- final_columns: float32 [16384, 16384], P('frame', 'pair')
- pair_grams: float32 [2, 512, 32, 512], P(None, 'frame', 'pair')
The draws below stay inside these ranges and needn't reach their ends.
Inputs may be any that keep to these rules, and one draw needn't show every extreme that they name: Each plan[s, h, :] is a permutation of 0 to 3. Each rotations[s, p] is the identity plus a random perturbation, well conditioned.
All inputs are finite; a program needn't handle non-finite values.
Results may differ from the reference program's by a relative error of at most 0.0001.
Values sent between devices are 32-bit elements; how exact they have to be, the bound alone decides.
No kernel may reach another device: no remote copies, remote signals or barrier semaphores. Data moves between devices by JAX's collectives and lax.ppermute only.
A program may use at most 320 MiB of HBM per device.

```python
import jax
import jax.numpy as jnp
from jax import lax

BW = 256
PAIRS_DEV = 2
STEPS = 2
M = 16384
NPAIRS = 32
NCOL = 16384


def draw_columns(key, part):
    key = jax.random.fold_in(key, 1)
    key_noise, key_common, key_scale = jax.random.split(key, 3)
    noise = jax.random.normal(key_noise, (M, NCOL + 1), jnp.float32)
    common = 0.6 * jax.random.normal(key_common, (M, 1), jnp.float32)
    spread = jnp.log(10.0)
    local_part = noise[:, :-1] + 0.8 * noise[:, 1:]
    column_scale = jnp.exp(jax.random.uniform(key_scale, (1, NCOL), jnp.float32, 0.0, 1.0) * spread)
    row_scale = 1.0 + 2.0 * jnp.arange(M, dtype=jnp.float32)[:, None] / M
    return ((local_part + common) * column_scale * row_scale).astype(jnp.float32)


def draw_rotations(key, part):
    key = jax.random.fold_in(key, 2)
    shape = (STEPS, NPAIRS, 2 * BW, 2 * BW)
    noise = jax.random.normal(key, shape, jnp.float32)
    identity = jnp.eye(2 * BW, dtype=jnp.float32)
    return (identity + 0.6 * noise / jnp.sqrt(jnp.float32(2 * BW))).astype(jnp.float32)


def draw_plan(key, part):
    key = jax.random.fold_in(key, 3)
    count = STEPS * (NPAIRS // PAIRS_DEV)
    keys = jax.random.split(key, count)
    orders = jax.vmap(lambda one_key: jax.random.permutation(one_key, 2 * PAIRS_DEV))(keys)
    return orders.reshape(STEPS, NPAIRS // PAIRS_DEV, 2 * PAIRS_DEV).astype(jnp.int32)


def setup_inputs(seed: int = 0) -> dict:
    key_list = jax.random.split(jax.random.key(seed), 4)
    return {
        "columns": draw_columns(jax.random.fold_in(key_list[3], 71), 0),
        "rotations": draw_rotations(jax.random.fold_in(key_list[3], 71), 0),
        "plan": draw_plan(jax.random.fold_in(key_list[3], 71), 0),
    }


epsilon = 1e-06

def reference(columns, rotations, plan):
    total = columns.shape[0]
    holders = NPAIRS // PAIRS_DEV
    held = columns.reshape(total, holders, 2 * PAIRS_DEV, BW)
    slot_ids = jnp.arange(2 * PAIRS_DEV, dtype=jnp.int32)
    grams_list = []
    for step in range(STEPS):
        selector = (plan[step][:, :, None] == slot_ids[None, None, :]).astype(jnp.float32)
        arranged = jnp.einsum('hks,rhsc->rhkc', selector, held, precision=lax.Precision.HIGHEST)
        paired = arranged.reshape(total, NPAIRS, 2 * BW)
        gram = jnp.einsum('rpi,rpj->pij', paired, paired, precision=lax.Precision.HIGHEST)
        diagonal_sq = jnp.diagonal(gram, axis1=1, axis2=2)
        scale = jnp.sqrt(jnp.float32(total)) * lax.rsqrt(diagonal_sq + epsilon)
        correlation = gram * scale[:, :, None] * scale[:, None, :] / total
        rotation = rotations[step]
        left_part = jnp.einsum('pki,pkj->pij', rotation, correlation, precision=lax.Precision.HIGHEST)
        turned = jnp.einsum('pik,pkj->pij', left_part, rotation, precision=lax.Precision.HIGHEST)
        grams_list.append(jnp.transpose(turned, (1, 0, 2)))
        updated = jnp.einsum('rpi,pij->rpj', paired * scale[None], rotation, precision=lax.Precision.HIGHEST)
        slots = updated.reshape(total, holders, 2 * PAIRS_DEV, BW)
        held = jnp.stack([slots[:, :, 0], slots[:, :, 2], jnp.roll(slots[:, :, 1], 1, axis=1), jnp.roll(slots[:, :, 3], -1, axis=1)], axis=2)
    return (held.reshape(total, NCOL), jnp.stack(grams_list))
```

```python
import functools

import jax
import jax.numpy as jnp
from jax import lax
from jax.experimental import pallas as pl
from jax.experimental.pallas import tpu as pltpu
from jax.sharding import PartitionSpec as P

BW = 256
STEPS = 2
PARTS = 2
CHUNK = 256
VMEM = 48 * 1024 * 1024

epsilon = 1e-06


def params(grid_dims=1):
    return pltpu.CompilerParams(
        dimension_semantics=("arbitrary",) * grid_dims, vmem_limit_bytes=VMEM
    )


def split(x):
    high = x.astype(jnp.bfloat16)
    low = (x - high.astype(jnp.float32)).astype(jnp.bfloat16)
    return high, low


def dot(a, b):
    return jnp.dot(a, b, preferred_element_type=jnp.float32)


def add_squares(acc, slot, x):
    rows, cols = x.shape
    for half in range(cols // 128):
        piece = x[:, half * 128 : (half + 1) * 128]
        squares = (piece * piece).reshape(rows // 8, 8, 128)
        acc[2 * slot + half] += jnp.sum(squares, axis=0)


def put_sums(sums_ref, acc):
    for row in range(8):
        sums_ref[row : row + 1, :] = jnp.sum(acc[row], axis=0, keepdims=True)


def squares_kernel(x_ref, sums_ref, acc):
    @pl.when(pl.program_id(0) == 0)
    def _():
        acc[...] = jnp.zeros_like(acc)

    for slot in range(4):
        add_squares(acc, slot, x_ref[:, slot * BW : (slot + 1) * BW])

    @pl.when(pl.program_id(0) == pl.num_programs(0) - 1)
    def _():
        put_sums(sums_ref, acc)


def squares(columns):
    rows, cols = columns.shape
    return pl.pallas_call(
        squares_kernel,
        grid=(rows // CHUNK,),
        in_specs=[pl.BlockSpec((CHUNK, cols), lambda i: (i, 0))],
        out_specs=pl.BlockSpec((8, 128), lambda i: (0, 0)),
        out_shape=jax.ShapeDtypeStruct((8, 128), jnp.float32),
        scratch_shapes=[pltpu.VMEM((8, 8, 128), jnp.float32)],
        compiler_params=params(),
        cost_estimate=pl.CostEstimate(
            flops=2 * rows * cols, bytes_accessed=4 * rows * cols, transcendentals=0
        ),
    )(columns)


def scaled_parts(total_rows, plan_ref, x_refs, sums_ref, high, low):
    scale = jnp.sqrt(jnp.float32(total_rows)) * lax.rsqrt(sums_ref[...] + epsilon)
    for slot in range(4):
        place = jnp.int32(0)
        for k in range(4):
            place += jnp.where(plan_ref[k] == slot, k, 0)
        for half in range(2):
            lanes = slice(half * 128, (half + 1) * 128)
            row = 2 * slot + half
            x = x_refs[slot][:, lanes] * scale[row : row + 1, :]
            h, l = split(x)
            high[place, :, lanes] = h
            low[place, :, lanes] = l


def rotate(pair, high, low, rot_high, rot_low):
    out = None
    for k in range(2):
        h, l = high[2 * pair + k], low[2 * pair + k]
        rows = slice(k * BW, (k + 1) * BW)
        rh, rl = rot_high[pair, rows, :], rot_low[pair, rows, :]
        term = dot(h, rh) + dot(l, rh) + dot(h, rl)
        out = term if out is None else out + term
    return out


def send_kernel(total_rows, plan_ref, x0, x1, x2, x3, sums_ref, rot_ref, up_ref, down_ref,
                high, low, rot_high, rot_low):
    @pl.when(pl.program_id(0) == 0)
    def _():
        for pair in range(2):
            rot_high[pair], rot_low[pair] = split(rot_ref[pair])

    scaled_parts(total_rows, plan_ref, (x0, x1, x2, x3), sums_ref, high, low)
    up_ref[...] = rotate(0, high, low, rot_high, rot_low)
    down_ref[...] = rotate(1, high, low, rot_high, rot_low)


def keep_kernel(total_rows, plan_ref, x0, x1, x2, x3, sums_ref, rot_ref, up_ref, down_ref,
                out_ref, new_sums_ref, high, low, rot_high, rot_low, acc):
    @pl.when(pl.program_id(0) == 0)
    def _():
        acc[...] = jnp.zeros_like(acc)
        for pair in range(2):
            rot_high[pair], rot_low[pair] = split(rot_ref[pair])

    scaled_parts(total_rows, plan_ref, (x0, x1, x2, x3), sums_ref, high, low)
    for pair, sent in ((0, up_ref), (1, down_ref)):
        kept = rotate(pair, high, low, rot_high, rot_low)
        out_ref[:, pair * BW : (pair + 1) * BW] = kept
        add_squares(acc, 2 * pair, kept)
        add_squares(acc, 2 * pair + 1, sent[...])

    @pl.when(pl.program_id(0) == pl.num_programs(0) - 1)
    def _():
        put_sums(new_sums_ref, acc)


def x_spec(row0, col):
    return pl.BlockSpec((CHUNK, BW), lambda i, plan: (i + row0, col))


def scratch():
    return [
        pltpu.VMEM((4, CHUNK, BW), jnp.bfloat16),
        pltpu.VMEM((4, CHUNK, BW), jnp.bfloat16),
        pltpu.VMEM((2, 2 * BW, BW), jnp.bfloat16),
        pltpu.VMEM((2, 2 * BW, BW), jnp.bfloat16),
    ]


def send_part(total_rows, rows, xs, specs, sums, rotation, plan):
    shape = jax.ShapeDtypeStruct((rows, BW), jnp.float32)
    return pl.pallas_call(
        functools.partial(send_kernel, total_rows),
        grid_spec=pltpu.PrefetchScalarGridSpec(
            num_scalar_prefetch=1,
            grid=(rows // CHUNK,),
            in_specs=specs
            + [
                pl.BlockSpec((8, 128), lambda i, plan: (0, 0)),
                pl.BlockSpec((2, 2 * BW, BW), lambda i, plan: (0, 0, 1)),
            ],
            out_specs=[pl.BlockSpec((CHUNK, BW), lambda i, plan: (i, 0))] * 2,
            scratch_shapes=scratch(),
        ),
        out_shape=[shape, shape],
        compiler_params=params(),
        cost_estimate=pl.CostEstimate(
            flops=3 * 2 * rows * 2 * BW * 2 * BW,
            bytes_accessed=4 * rows * 6 * BW,
            transcendentals=0,
        ),
    )(plan, *xs, sums, rotation)


def keep_part(total_rows, rows, out_cols, xs, specs, sums, rotation, plan, up, down):
    return pl.pallas_call(
        functools.partial(keep_kernel, total_rows),
        grid_spec=pltpu.PrefetchScalarGridSpec(
            num_scalar_prefetch=1,
            grid=(rows // CHUNK,),
            in_specs=specs
            + [
                pl.BlockSpec((8, 128), lambda i, plan: (0, 0)),
                pl.BlockSpec((2, 2 * BW, BW), lambda i, plan: (0, 0, 0)),
                pl.BlockSpec((CHUNK, BW), lambda i, plan: (i, 0)),
                pl.BlockSpec((CHUNK, BW), lambda i, plan: (i, 0)),
            ],
            out_specs=[
                pl.BlockSpec((CHUNK, 2 * BW), lambda i, plan: (i, 0)),
                pl.BlockSpec((8, 128), lambda i, plan: (0, 0)),
            ],
            scratch_shapes=scratch() + [pltpu.VMEM((8, 8, 128), jnp.float32)],
        ),
        out_shape=[
            jax.ShapeDtypeStruct((rows, out_cols), jnp.float32),
            jax.ShapeDtypeStruct((8, 128), jnp.float32),
        ],
        compiler_params=params(),
        cost_estimate=pl.CostEstimate(
            flops=3 * 2 * rows * 2 * BW * 2 * BW,
            bytes_accessed=4 * rows * 8 * BW,
            transcendentals=0,
        ),
    )(plan, *xs, sums, rotation, up, down)


def gram_kernel(total_rows, k_ref, up_ref, down_ref, gram_ref, square, cross):
    @pl.when(pl.program_id(0) == 0)
    def _():
        square[...] = jnp.zeros_like(square)
        cross[...] = jnp.zeros_like(cross)

    for pair, sent in ((0, up_ref), (1, down_ref)):
        ah, al = split(k_ref[:, pair * BW : (pair + 1) * BW])
        bh, bl = split(sent[...])
        at, bt = ah.T, bh.T
        square[pair, 0] += dot(at, ah)
        square[pair, 1] += dot(at, bh)
        square[pair, 2] += dot(bt, bh)
        cross[pair, 0] += dot(at, al)
        cross[pair, 1] += dot(at, bl)
        cross[pair, 2] += dot(bt, al)
        cross[pair, 3] += dot(bt, bl)

    @pl.when(pl.program_id(0) == pl.num_programs(0) - 1)
    def _():
        inverse = jnp.float32(1.0 / total_rows)
        for pair in range(2):
            aa = (square[pair, 0] + (cross[pair, 0] + cross[pair, 0].T)) * inverse
            ab = (square[pair, 1] + (cross[pair, 1] + cross[pair, 2].T)) * inverse
            bb = (square[pair, 2] + (cross[pair, 3] + cross[pair, 3].T)) * inverse
            gram_ref[pair, :BW, :BW] = aa
            gram_ref[pair, :BW, BW:] = ab
            gram_ref[pair, BW:, :BW] = ab.T
            gram_ref[pair, BW:, BW:] = bb


def gram(total_rows, kept, up, down):
    rows = kept.shape[0]
    return pl.pallas_call(
        functools.partial(gram_kernel, total_rows),
        grid=(rows // CHUNK,),
        in_specs=[
            pl.BlockSpec((CHUNK, 2 * BW), lambda i: (i, 0)),
            pl.BlockSpec((CHUNK, BW), lambda i: (i, 0)),
            pl.BlockSpec((CHUNK, BW), lambda i: (i, 0)),
        ],
        out_specs=pl.BlockSpec((2, 2 * BW, 2 * BW), lambda i: (0, 0, 0)),
        out_shape=jax.ShapeDtypeStruct((2, 2 * BW, 2 * BW), jnp.float32),
        scratch_shapes=[
            pltpu.VMEM((2, 3, BW, BW), jnp.float32),
            pltpu.VMEM((2, 4, BW, BW), jnp.float32),
        ],
        compiler_params=params(),
        cost_estimate=pl.CostEstimate(
            flops=2 * 2 * rows * 7 * BW * BW, bytes_accessed=4 * rows * 4 * BW, transcendentals=0
        ),
    )(kept, up, down)


def fill_kernel(_, up_ref, down_ref, out_ref):
    out_ref[:, :BW] = up_ref[...]
    out_ref[:, BW:] = down_ref[...]


def fill(out, up, down, row0):
    rows = up.shape[0]
    first = row0 // CHUNK
    return pl.pallas_call(
        fill_kernel,
        grid=(rows // CHUNK,),
        in_specs=[
            pl.BlockSpec(memory_space=pl.ANY),
            pl.BlockSpec((CHUNK, BW), lambda i: (i, 0)),
            pl.BlockSpec((CHUNK, BW), lambda i: (i, 0)),
        ],
        out_specs=pl.BlockSpec((CHUNK, 2 * BW), lambda i: (i + first, 1)),
        out_shape=jax.ShapeDtypeStruct(out.shape, out.dtype),
        input_output_aliases={0: 0},
        compiler_params=params(),
        cost_estimate=pl.CostEstimate(
            flops=0, bytes_accessed=4 * rows * 4 * BW, transcendentals=0
        ),
    )(out, up, down)


def shift(x, by):
    size = lax.axis_size("pair")
    return lax.ppermute(x, "pair", [(i, (i + by) % size) for i in range(size)])


def swap(x, bit):
    size = lax.axis_size("frame")
    return lax.ppermute(x, "frame", [(i, i ^ bit) for i in range(size)])


def all_sum(x):
    bit = 1
    while bit < lax.axis_size("frame"):
        x = x + swap(x, bit)
        bit *= 2
    return x


def scatter_sum(g):
    frames = lax.axis_size("frame")
    width = 2 * BW // frames
    me = lax.axis_index("frame")
    total = lax.dynamic_slice_in_dim(g, me * width, width, 1)
    for k in range(1, frames):
        total = total + swap(lax.dynamic_slice_in_dim(g, (me ^ k) * width, width, 1), k)
    return jnp.transpose(total, (1, 0, 2))


def local(columns, rotations, plan):
    rows = columns.shape[0]
    total_rows = rows * lax.axis_size("frame")
    part = rows // PARTS
    tile = all_sum(squares(columns))

    def x_of(step, row0, count):
        first = row0 // CHUNK
        if step == 0:
            return [columns] * 4, [x_spec(first, slot) for slot in range(4)]
        kept, ups, downs = held
        return (
            [kept, kept, ups[row0 // part], downs[row0 // part]],
            [x_spec(first, 0), x_spec(first, 1), x_spec(0, 0), x_spec(0, 0)],
        )

    held = None
    grams_list = []
    for step in range(STEPS):
        ups, downs, got_up, got_down = [], [], [], []
        for p in range(PARTS):
            xs, specs = x_of(step, p * part, part)
            up, down = send_part(total_rows, part, xs, specs, tile, rotations[step], plan[step, 0])
            ups.append(up)
            downs.append(down)
            got_up.append(shift(up, 1))
            got_down.append(shift(down, -1))
        return_up = jnp.concatenate(ups)
        return_down = jnp.concatenate(downs)
        if step == 0:
            xs, specs = x_of(step, 0, rows)
        else:
            kept, a, b = held
            xs = [kept, kept, jnp.concatenate(a), jnp.concatenate(b)]
            specs = [x_spec(0, 0), x_spec(0, 1), x_spec(0, 0), x_spec(0, 0)]
        last = step == STEPS - 1
        kept, sums = keep_part(
            total_rows, rows, (4 if last else 2) * BW, xs, specs, tile, rotations[step],
            plan[step, 0], return_up, return_down,
        )
        if not last:
            before, after = shift(sums, 1), shift(sums, -1)
            tile = all_sum(jnp.concatenate([sums[0:2], sums[4:6], before[2:4], after[6:8]]))
        grams_list.append(scatter_sum(gram(total_rows, kept, return_up, return_down)))
        held = (kept, got_up, got_down)
    out, ups, downs = held
    for p in range(PARTS):
        out = fill(out, ups[p], downs[p], p * part)
    return out, jnp.stack(grams_list)


def solution(mesh):
    in_specs = (P("frame", "pair"), P(None, "pair", None, None), P(None, "pair", None))
    out_specs = (P("frame", "pair"), P(None, "frame", "pair", None))
    return jax.shard_map(local, mesh=mesh, in_specs=in_specs, out_specs=out_specs, check_vma=False)
```

```python
import functools

import jax
import jax.numpy as jnp
from jax import lax
from jax.experimental import pallas as pl
from jax.experimental.pallas import tpu as pltpu
from jax.sharding import PartitionSpec as P

BW = 256
STEPS = 2
FIRST_PART = 12
READ = 256
CHUNK = 768
VMEM = 16 * 1024 * 1024

epsilon = 1e-06

in_vmem = pl.BlockSpec(memory_space=pltpu.VMEM)
in_smem = pl.BlockSpec(memory_space=pltpu.SMEM)
in_hbm = pl.BlockSpec(memory_space=pltpu.HBM)
anywhere = pl.BlockSpec(memory_space=pl.ANY)


def f32(*shape):
    return jax.ShapeDtypeStruct(shape, jnp.float32)


def bf16(*shape):
    return jax.ShapeDtypeStruct(shape, jnp.bfloat16)


def params(limit=VMEM):
    return pltpu.CompilerParams(vmem_limit_bytes=limit)


def cost(flops, nbytes):
    return pl.CostEstimate(flops=flops, bytes_accessed=nbytes, transcendentals=0)


def split(x):
    high = x.astype(jnp.bfloat16)
    low = (x - high.astype(jnp.float32)).astype(jnp.bfloat16)
    return high, low


def add_squares(acc, slot, x):
    rows, cols = x.shape
    for half in range(cols // 128):
        piece = x[:, half * 128 : (half + 1) * 128]
        acc[2 * slot + half] += jnp.sum((piece * piece).reshape(rows // 8, 8, 128), axis=0)


def put_sums(sums_ref, acc):
    for row in range(8):
        sums_ref[row : row + 1, :] = jnp.sum(acc[row], axis=0, keepdims=True)


def first_kernel(x_ref, high_ref, low_ref, sums_ref, x, sem, acc):
    rows = x_ref.shape[0]
    copies = []
    for i in range(rows // READ):
        here = pl.ds(i * READ, READ)
        copies.append(pltpu.make_async_copy(x_ref.at[here, :], x.at[here, :], sem.at[i]))
    for copy in copies:
        copy.start()
    acc[...] = jnp.zeros_like(acc)
    for i, copy in enumerate(copies):
        here = slice(i * READ, (i + 1) * READ)
        copy.wait()
        for slot in range(4):
            piece = x[here, slot * BW : (slot + 1) * BW]
            add_squares(acc, slot, piece)
            high_ref[slot, here, :], low_ref[slot, here, :] = split(piece)
    put_sums(sums_ref, acc)


def first(columns):
    rows, cols = columns.shape
    return pl.pallas_call(
        first_kernel,
        in_specs=[in_hbm],
        out_specs=[in_vmem] * 3,
        out_shape=[bf16(4, rows, BW), bf16(4, rows, BW), f32(8, 128)],
        scratch_shapes=[
            pltpu.VMEM((rows, cols), jnp.float32),
            pltpu.SemaphoreType.DMA((rows // READ,)),
            pltpu.VMEM((8, 8, 128), jnp.float32),
        ],
        compiler_params=params(44 * 1024 * 1024),
        cost_estimate=cost(1 << 10, 1 << 10),
        name="first",
    )(columns)


def scale_kernel(total_rows, step, plan_ref, sums_ref, rot_ref, out_ref, scratch):
    scratch[...] = jnp.sqrt(jnp.float32(total_rows)) * lax.rsqrt(sums_ref[...] + epsilon)
    for k in range(4):
        pair, half = k // 2, k % 2
        for part in range(2):
            row = scratch[pl.ds(2 * plan_ref[step, 0, k] + part, 1), :]
            column = jnp.broadcast_to(row, (128, 128)).T
            top = half * BW + part * 128
            for c in range(4):
                lanes = slice(c * 128, (c + 1) * 128)
                h, l = split(rot_ref[step, pair, top : top + 128, lanes] * column)
                out_ref[pair, top : top + 128, lanes] = h
                out_ref[pair, 2 * BW + top : 2 * BW + top + 128, lanes] = h
                out_ref[pair, 4 * BW + top : 4 * BW + top + 128, lanes] = l


def scaled(total_rows, step, sums, rotations, plan):
    return pl.pallas_call(
        functools.partial(scale_kernel, total_rows, step),
        in_specs=[in_smem, in_vmem, in_vmem],
        out_specs=in_vmem,
        out_shape=bf16(2, 6 * BW, 2 * BW),
        scratch_shapes=[pltpu.VMEM((8, 128), jnp.float32)],
        compiler_params=params(),
        cost_estimate=cost(1 << 10, 1 << 10),
        name="scale",
    )(plan, sums, rotations)


def pieces(rows):
    count = -(-rows // CHUNK)
    return [(k * (rows // count), rows // count) for k in range(count)]


def stacked(high_ref, low_ref, plan_ref, step, pair, row, count):
    slots = [plan_ref[step, 0, 2 * pair + k] for k in range(2)]
    h = [high_ref[slot, row : row + count, :] for slot in slots]
    l = [low_ref[slot, row : row + count, :] for slot in slots]
    return jnp.concatenate(h + l + h, axis=1)


def half_gram(nh, nl):
    turned = nh.T
    return jnp.dot(
        jnp.concatenate([turned, turned], axis=1),
        jnp.concatenate([nh * jnp.bfloat16(0.5), nl], axis=0),
        preferred_element_type=jnp.float32,
    )


def cut_gram(total_rows, gram_acc, outs):
    for pair in range(2):
        half = gram_acc[pair]
        gram_acc[pair] = (half + half.T) * jnp.float32(1.0 / total_rows)
    x = lax.axis_index("frame") // 2
    near = x + 1 - 2 * (x % 2)
    blocks = ((x, 3 - x), (near, 3 - near)), ((x, near), (3 - x, 3 - near))
    for pair in range(2):
        for which in range(2):
            for k in range(2):
                row = pl.multiple_of(128 * blocks[pair][which][k], 128)
                outs[2 * pair + which][k] = gram_acc[pair, pl.ds(row, 128), :]


cut_shapes = [f32(2, 128, 2 * BW)] * 4


def send_kernel(parts, plan_ref, high_ref, low_ref, rot_ref, *refs):
    outs, acc = refs[:-1], refs[-1]
    acc[...] = jnp.zeros_like(acc)
    first_row = 0
    for p, rows in enumerate(parts):
        for r, count in pieces(rows):
            for pair in range(2):
                x = stacked(high_ref, low_ref, plan_ref, 0, pair, first_row + r, count)
                new = jnp.dot(x, rot_ref[pair, :, BW:], preferred_element_type=jnp.float32)
                outs[2 * p + pair][r : r + count, :] = new
                add_squares(acc, pair, new)
        first_row += rows
    for pair in range(2):
        top = parts[0]
        for half in range(2):
            lanes = slice(half * 128, (half + 1) * 128)
            outs[pair][top : top + 8, lanes] = acc[2 * pair + half]


def send(parts, plan, high, low, rot):
    extra = [8] + [0] * (len(parts) - 1)
    outs = [f32(rows + more, BW) for rows, more in zip(parts, extra) for _ in range(2)]
    outs = pl.pallas_call(
        functools.partial(send_kernel, parts),
        in_specs=[in_smem] + [in_vmem] * 3,
        out_specs=[in_vmem] * len(outs),
        out_shape=outs,
        scratch_shapes=[pltpu.VMEM((4, 8, 128), jnp.float32)],
        compiler_params=params(),
        cost_estimate=cost(1 << 10, 1 << 10),
        name="send",
    )(plan, high, low, rot)
    return outs[0::2], outs[1::2]


def stay_kernel(parts, plan_ref, high_ref, low_ref, rot_ref, *refs):
    outs, sums_ref, acc = refs[4:-2], refs[-2], refs[-1]
    acc[...] = jnp.zeros_like(acc)
    first_row = 0
    for p, rows in enumerate(parts):
        for r, count in pieces(rows):
            for pair in range(2):
                x = stacked(high_ref, low_ref, plan_ref, 0, pair, first_row + r, count)
                new = jnp.dot(x, rot_ref[pair, :, :BW], preferred_element_type=jnp.float32)
                h, l = split(new)
                outs[2 * p][pair, r : r + count, :] = h
                outs[2 * p + 1][pair, r : r + count, :] = l
                add_squares(acc, pair, new)
        first_row += rows
    for row in range(4):
        sums_ref[row : row + 1, :] = jnp.sum(acc[row], axis=0, keepdims=True)
    sums_ref[4:8] = jnp.zeros((4, 128), jnp.float32)


def stay(parts, plan, high, low, rot, up, down):
    outs = [up, down]
    outs += [bf16(2, rows, BW) for rows in parts for _ in range(2)] + [f32(8, 128)]
    outs = pl.pallas_call(
        functools.partial(stay_kernel, parts),
        in_specs=[in_smem] + [in_vmem] * 3 + [anywhere] * 2,
        out_specs=[anywhere] * 2 + [in_vmem] * (len(outs) - 2),
        out_shape=[jax.ShapeDtypeStruct(out.shape, out.dtype) for out in outs],
        input_output_aliases={4: 0, 5: 1},
        scratch_shapes=[pltpu.VMEM((4, 8, 128), jnp.float32)],
        compiler_params=params(),
        cost_estimate=cost(1 << 10, 1 << 10),
        name="stay",
    )(plan, high, low, rot, up, down)
    return list(zip(outs[2:-1:2], outs[3:-1:2])), outs[-1], outs[0], outs[1]


def gram_kernel(parts, *refs):
    ins, gram_acc = refs[:-1], refs[-1]
    for p, rows in enumerate(parts):
        kept_high, kept_low, up, down = ins[4 * p : 4 * p + 4]
        for r, count in pieces(rows):
            here = slice(r, r + count)
            for pair, sent in ((0, up), (1, down)):
                h, l = split(sent[here, :])
                gram = half_gram(
                    jnp.concatenate([kept_high[pair, here, :], h], axis=1),
                    jnp.concatenate([kept_low[pair, here, :], l], axis=1),
                )
                gram_acc[pair] = gram if p + r == 0 else gram + gram_acc[pair]


def gram(parts, kept, ups, downs):
    args = []
    for k, up, down in zip(kept, ups, downs):
        args += [*k, up, down]
    return pl.pallas_call(
        functools.partial(gram_kernel, parts),
        in_specs=[in_vmem] * len(args),
        out_specs=in_vmem,
        out_shape=f32(2, 2 * BW, 2 * BW),
        compiler_params=params(),
        cost_estimate=cost(1 << 10, 1 << 10),
        name="gram",
    )(*args)


def cut_kernel(total_rows, gram_ref, *refs):
    outs, gram_acc = refs[-5:-1], refs[-1]
    gram_acc[...] = gram_ref[...]
    cut_gram(total_rows, gram_acc, outs)


def cut(total_rows, half, after, later=()):
    shapes = [jax.ShapeDtypeStruct(x.shape, x.dtype) for x in later]
    count = len(later)
    outs = pl.pallas_call(
        functools.partial(cut_kernel, total_rows),
        in_specs=[in_vmem] + [anywhere] * (count + len(after)),
        out_specs=[anywhere] * count + [in_vmem] * 4,
        out_shape=shapes + cut_shapes,
        input_output_aliases={1 + k: k for k in range(count)},
        scratch_shapes=[pltpu.VMEM((2, 2 * BW, 2 * BW), jnp.float32)],
        compiler_params=params(),
        cost_estimate=cost(1 << 10, 1 << 10),
        name="cut",
    )(half, *later, *after)
    return outs[count:], outs[:count]


def update_kernel(parts, part, plan_ref, kept_high, kept_low, up_in, down_in,
                  rot_ref, *refs):
    refs = list(refs)
    if part:
        gram_in = refs.pop(0)
        refs.pop(0)
    result, out_up, out_down = refs.pop(0), refs.pop(0), refs.pop(0)
    gram_acc = refs.pop(0)
    high_ref, low_ref, kept_ref, sem = refs
    rows, top = parts[part], sum(parts[:part])
    for slot in range(2):
        high_ref[slot] = kept_high[slot]
        low_ref[slot] = kept_low[slot]
    high_ref[2], low_ref[2] = split(up_in[:rows, :])
    high_ref[3], low_ref[3] = split(down_in[:rows, :])

    copies = []
    for k, (r, count) in enumerate(pieces(rows)):
        here = slice(r, r + count)
        for pair, sent in ((0, out_up), (1, out_down)):
            x = stacked(high_ref, low_ref, plan_ref, 1, pair, r, count)
            new = jnp.dot(x, rot_ref[pair], preferred_element_type=jnp.float32)
            kept_ref[here, pair * BW : (pair + 1) * BW] = new[:, :BW]
            sent[here, :] = new[:, BW:]
            gram = half_gram(*split(new))
            if r:
                gram = gram + gram_acc[pair]
            elif part:
                gram = gram + gram_in[pair]
            gram_acc[pair] = gram
        copies.append(
            pltpu.make_async_copy(
                kept_ref.at[pl.ds(r, count), :],
                result.at[pl.ds(top + r, count), pl.ds(0, 2 * BW)],
                sem.at[k],
            )
        )
        copies[-1].start()
    for copy in copies:
        copy.wait()


def update(parts, part, plan, xs, rot, gram_in, result):
    rows = parts[part]
    args = [plan, *xs, rot]
    in_specs = [in_smem] + [in_vmem] * 5
    if part:
        args += [gram_in, result]
        in_specs += [in_vmem, in_hbm]
    outs = [f32(sum(parts), 4 * BW), f32(rows, BW), f32(rows, BW)]
    outs.append(f32(2, 2 * BW, 2 * BW))
    return pl.pallas_call(
        functools.partial(update_kernel, parts, part),
        in_specs=in_specs,
        out_specs=[in_hbm] + [in_vmem] * (len(outs) - 1),
        out_shape=outs,
        scratch_shapes=[
            pltpu.VMEM((4, rows, BW), jnp.bfloat16),
            pltpu.VMEM((4, rows, BW), jnp.bfloat16),
            pltpu.VMEM((rows, 2 * BW), jnp.float32),
            pltpu.SemaphoreType.DMA((len(pieces(rows)),)),
        ],
        input_output_aliases={len(args) - 1: 0} if part else {},
        compiler_params=params(),
        cost_estimate=cost(1 << 10, 1 << 10),
        name="update",
    )(*args)


def fill_kernel(row0, _, up, down, out, sem):
    rows = up.shape[0]
    copies = [
        pltpu.make_async_copy(
            ref, out.at[pl.ds(row0, rows), pl.ds((2 + k) * BW, BW)], sem.at[k]
        )
        for k, ref in enumerate((up, down))
    ]
    for copy in copies:
        copy.start()
    for copy in copies:
        copy.wait()


def fill(out, up, down, row0):
    return pl.pallas_call(
        functools.partial(fill_kernel, row0),
        in_specs=[in_hbm, in_vmem, in_vmem],
        out_specs=in_hbm,
        out_shape=jax.ShapeDtypeStruct(out.shape, out.dtype),
        input_output_aliases={0: 0},
        scratch_shapes=[pltpu.SemaphoreType.DMA((2,))],
        compiler_params=params(),
        cost_estimate=cost(1 << 10, 1 << 10),
        name="fill",
    )(out, up, down)


def mix_kernel(top, own, before, after, _, out):
    out[0:4] = own[0:4]
    for k, ref in enumerate((before, after)):
        for half in range(2):
            row = 4 + 2 * k + half
            lanes = slice(half * 128, (half + 1) * 128)
            out[row : row + 1, :] = jnp.sum(ref[top : top + 8, lanes], axis=0, keepdims=True)


def mix(top, own, before, after, done):
    return pl.pallas_call(
        functools.partial(mix_kernel, top),
        in_specs=[in_vmem] * 3 + [anywhere],
        out_specs=in_vmem,
        out_shape=f32(8, 128),
        compiler_params=params(),
        cost_estimate=cost(1 << 10, 1 << 10),
        name="mix",
    )(own, before, after, done)


def add_kernel(mine0, got0, mine1, got1, *refs):
    keep_ref, send0, send1 = refs[-3:]
    for pair, (mine, got, sent) in enumerate(((mine0, got0, send0), (mine1, got1, send1))):
        keep_ref[pair] = mine[0] + got[0]
        sent[...] = mine[1] + got[1]


def add_first(args, after):
    block = f32(128, 2 * BW)
    return pl.pallas_call(
        add_kernel,
        in_specs=[in_vmem] * 4 + [anywhere] * len(after),
        out_specs=[in_vmem] * 3,
        out_shape=[f32(2, 128, 2 * BW), block, block],
        compiler_params=params(),
        cost_estimate=cost(1 << 10, 1 << 10),
        name="add",
    )(*args, *after)


def halve_kernel(mine, got0, got1, *refs):
    keep_ref, send_ref = refs[-2:]
    bit = lax.axis_index("frame") % 2
    for pair, got in enumerate((got0, got1)):
        for ref, chosen in ((keep_ref, bit), (send_ref, 1 - bit)):
            rows = pl.ds(pl.multiple_of(64 * chosen, 64), 64)
            ref[pair] = mine[pair, rows, :] + got[rows, :]


def halve(args, after):
    return pl.pallas_call(
        halve_kernel,
        in_specs=[in_vmem] * 3 + [anywhere] * len(after),
        out_specs=[in_vmem] * 2,
        out_shape=[f32(2, 64, 2 * BW)] * 2,
        compiler_params=params(),
        cost_estimate=cost(1 << 10, 1 << 10),
        name="halve",
    )(*args, *after)


def finish_kernel(row0, _, up, down, *refs):
    out, grams, sem = refs[-3:]
    rows = up.shape[0]
    copies = [
        pltpu.make_async_copy(
            ref, out.at[pl.ds(row0, rows), pl.ds((2 + k) * BW, BW)], sem.at[k]
        )
        for k, ref in enumerate((up, down))
    ]
    for copy in copies:
        copy.start()
    for step in range(STEPS):
        mine, got = refs[2 * step], refs[2 * step + 1]
        for pair in range(2):
            grams[step, :, pair, :] = mine[pair] + got[pair]
    for copy in copies:
        copy.wait()


def finish(out, up, down, row0, pieces):
    args = [array for piece in pieces for array in piece]
    return pl.pallas_call(
        functools.partial(finish_kernel, row0),
        in_specs=[in_hbm] + [in_vmem] * (2 + len(args)),
        out_specs=[in_hbm, in_vmem],
        out_shape=[
            jax.ShapeDtypeStruct(out.shape, out.dtype),
            f32(STEPS, 64, 2, 2 * BW),
        ],
        input_output_aliases={0: 0},
        scratch_shapes=[pltpu.SemaphoreType.DMA((2,))],
        compiler_params=params(),
        cost_estimate=cost(1 << 10, 1 << 10),
        name="finish",
    )(out, up, down, *args)


def shift(x, by):
    size = lax.axis_size("pair")
    return lax.ppermute(x, "pair", [(i, (i + by) % size) for i in range(size)])


def swap(x, bit):
    size = lax.axis_size("frame")
    return lax.ppermute(x, "frame", [(i, i ^ bit) for i in range(size)])


def all_sum(x, bits):
    for bit in bits:
        x = x + swap(x, bit)
    return x


def local(columns, rotations, plan):
    rows = columns.shape[0]
    total_rows = rows * lax.axis_size("frame")
    parts = (rows * FIRST_PART // 32, rows * (32 - FIRST_PART) // 32)
    high, low, sums = first(columns)
    rot = scaled(total_rows, 0, all_sum(sums, (2, 6, 1)), rotations, plan)
    ups, downs = send(parts, plan, high, low, rot)
    kept, own, late_up, late_down = stay(parts, plan, high, low, rot, ups[1], downs[1])
    ups, downs = (ups[0], late_up), (downs[0], late_down)
    moved = [(shift(up, 1), shift(down, -1)) for up, down in zip(ups, downs)]
    half = gram(parts, kept, ups, downs)
    mixed = mix(parts[0], own, *moved[0], half)
    tile = all_sum(mixed, (1, 6, 2))
    halves, _ = cut(total_rows, half, (mixed,))
    got = swap(halves[1], 2), swap(halves[3], 6)
    keep0, send0, send1 = add_first((halves[0], got[0], halves[2], got[1]), ())

    rot = scaled(total_rows, 1, tile, rotations, plan)
    half = result = None
    sent = []
    for p in range(len(parts)):
        result, up, down, half = update(
            parts, p, plan, (*kept[p], *moved[p]), rot, half, result
        )
        sent.append((up, down))
    early = shift(sent[0][0], 1), shift(sent[0][1], -1)

    second = halve((keep0, swap(send0, 6), swap(send1, 2)), ())
    halves, sent = cut(total_rows, half, (*early, second[0]), sent[1])
    late = shift(sent[0], 1), shift(sent[1], -1)
    got = swap(halves[1], 2), swap(halves[3], 6)
    first_grams = (second[0], swap(second[1], 1))
    keep0, send0, send1 = add_first((halves[0], got[0], halves[2], got[1]), ())
    second = halve((keep0, swap(send0, 6), swap(send1, 2)), ())
    last_grams = (second[0], swap(second[1], 1))
    result = fill(result, *early, 0)
    return finish(result, *late, parts[0], (first_grams, last_grams))


def solution(mesh):
    in_specs = (P("frame", "pair"), P(None, "pair", None, None), P(None, "pair", None))
    out_specs = (P("frame", "pair"), P(None, "frame", "pair", None))
    return jax.shard_map(local, mesh=mesh, in_specs=in_specs, out_specs=out_specs, check_vma=False)
```

```python
import functools

import jax
import jax.numpy as jnp
from jax import lax
from jax.experimental import pallas as pl
from jax.experimental.pallas import tpu as pltpu
from jax.sharding import PartitionSpec as P

BW = 256
STEPS = 2
READ = 256
CHUNK = 512
VMEM = 16 * 1024 * 1024

epsilon = 1e-06

in_vmem = pl.BlockSpec(memory_space=pltpu.VMEM)
in_smem = pl.BlockSpec(memory_space=pltpu.SMEM)
in_hbm = pl.BlockSpec(memory_space=pltpu.HBM)
anywhere = pl.BlockSpec(memory_space=pl.ANY)


def f32(*shape):
    return jax.ShapeDtypeStruct(shape, jnp.float32)


def bf16(*shape):
    return jax.ShapeDtypeStruct(shape, jnp.bfloat16)


def params(limit=VMEM):
    return pltpu.CompilerParams(vmem_limit_bytes=limit)


def cost(flops, nbytes):
    return pl.CostEstimate(flops=flops, bytes_accessed=nbytes, transcendentals=0)


def split(x):
    high = x.astype(jnp.bfloat16)
    low = (x - high.astype(jnp.float32)).astype(jnp.bfloat16)
    return high, low


def add_squares(acc, slot, x):
    rows, cols = x.shape
    for half in range(cols // 128):
        piece = x[:, half * 128 : (half + 1) * 128]
        acc[2 * slot + half] += jnp.sum((piece * piece).reshape(rows // 8, 8, 128), axis=0)


def put_sums(sums_ref, acc):
    for row in range(8):
        sums_ref[row : row + 1, :] = jnp.sum(acc[row], axis=0, keepdims=True)


def first_kernel(x_ref, high_ref, low_ref, sums_ref, x, sem, acc):
    rows = x_ref.shape[0]
    copies = []
    for i in range(rows // READ):
        here = pl.ds(i * READ, READ)
        copies.append(pltpu.make_async_copy(x_ref.at[here, :], x.at[here, :], sem.at[i]))
    for copy in copies:
        copy.start()
    acc[...] = jnp.zeros_like(acc)
    for i, copy in enumerate(copies):
        here = slice(i * READ, (i + 1) * READ)
        copy.wait()
        for slot in range(4):
            piece = x[here, slot * BW : (slot + 1) * BW]
            add_squares(acc, slot, piece)
            high_ref[slot, here, :], low_ref[slot, here, :] = split(piece)
    put_sums(sums_ref, acc)


def first(columns):
    rows, cols = columns.shape
    return pl.pallas_call(
        first_kernel,
        in_specs=[in_hbm],
        out_specs=[in_vmem] * 3,
        out_shape=[bf16(4, rows, BW), bf16(4, rows, BW), f32(8, 128)],
        scratch_shapes=[
            pltpu.VMEM((rows, cols), jnp.float32),
            pltpu.SemaphoreType.DMA((rows // READ,)),
            pltpu.VMEM((8, 8, 128), jnp.float32),
        ],
        compiler_params=params(44 * 1024 * 1024),
        cost_estimate=cost(1 << 10, 1 << 10),
        name="first",
    )(columns)


def scale_kernel(total_rows, step, plan_ref, here_ref, there_ref, rot_ref, *refs):
    out_ref, scratch = refs[-2:]
    sums = here_ref[...] + there_ref[...]
    scratch[...] = jnp.sqrt(jnp.float32(total_rows)) * lax.rsqrt(sums + epsilon)
    for k in range(4):
        pair, half = k // 2, k % 2
        for part in range(2):
            row = scratch[pl.ds(2 * plan_ref[step, 0, k] + part, 1), :]
            column = jnp.broadcast_to(row, (128, 128)).T
            top = half * BW + part * 128
            for c in range(4):
                lanes = slice(c * 128, (c + 1) * 128)
                h, l = split(rot_ref[step, pair, top : top + 128, lanes] * column)
                out_ref[pair, top : top + 128, lanes] = h
                out_ref[pair, 2 * BW + top : 2 * BW + top + 128, lanes] = h
                out_ref[pair, 4 * BW + top : 4 * BW + top + 128, lanes] = l


def scaled(total_rows, step, sums, rotations, plan, after=()):
    return pl.pallas_call(
        functools.partial(scale_kernel, total_rows, step),
        in_specs=[in_smem] + [in_vmem] * 3 + [anywhere] * len(after),
        out_specs=in_vmem,
        out_shape=bf16(2, 6 * BW, 2 * BW),
        scratch_shapes=[pltpu.VMEM((8, 128), jnp.float32)],
        compiler_params=params(),
        cost_estimate=cost(1 << 10, 1 << 10),
        name="scale",
    )(plan, *sums, rotations, *after)


def pieces(rows):
    count = -(-rows // CHUNK)
    return [(k * (rows // count), rows // count) for k in range(count)]


def stacked(high_ref, low_ref, plan_ref, step, pair, row, count):
    slots = [plan_ref[step, 0, 2 * pair + k] for k in range(2)]
    h = [high_ref[slot, row : row + count, :] for slot in slots]
    l = [low_ref[slot, row : row + count, :] for slot in slots]
    return jnp.concatenate(h + l + h, axis=1)


def half_gram(nh, nl):
    turned = nh.T
    return jnp.dot(
        jnp.concatenate([turned, turned], axis=1),
        jnp.concatenate([nh * jnp.bfloat16(0.5), nl], axis=0),
        preferred_element_type=jnp.float32,
    )


def cut_gram(total_rows, pair, gram_acc, mine, other):
    half = gram_acc[pair]
    gram_acc[pair] = (half + half.T) * jnp.float32(1.0 / total_rows)
    x = lax.axis_index("frame") // 2
    near = x + 1 - 2 * (x % 2)
    blocks = (((x, 3 - x), (near, 3 - near)), ((x, near), (3 - x, 3 - near)))[pair]
    for ref, rows in zip((mine, other), blocks):
        for k in range(2):
            row = pl.multiple_of(128 * rows[k], 128)
            ref[k] = gram_acc[pair, pl.ds(row, 128), :]


def send_kernel(plan_ref, high_ref, low_ref, rot_ref, up, down, up_sums, down_sums, acc):
    acc[...] = jnp.zeros_like(acc)
    for r, count in pieces(up.shape[0]):
        for pair, sent in enumerate((up, down)):
            x = stacked(high_ref, low_ref, plan_ref, 0, pair, r, count)
            new = jnp.dot(x, rot_ref[pair, :, BW:], preferred_element_type=jnp.float32)
            sent[r : r + count, :] = new
            add_squares(acc, pair, new)
    for pair, sums in enumerate((up_sums, down_sums)):
        for half in range(2):
            sums[:, half * 128 : (half + 1) * 128] = acc[2 * pair + half]


def send(plan, high, low, rot):
    rows = high.shape[1]
    return pl.pallas_call(
        send_kernel,
        in_specs=[in_smem] + [in_vmem] * 3,
        out_specs=[in_vmem] * 4,
        out_shape=[f32(rows, BW)] * 2 + [f32(8, BW)] * 2,
        scratch_shapes=[pltpu.VMEM((4, 8, 128), jnp.float32)],
        compiler_params=params(),
        cost_estimate=cost(1 << 10, 1 << 10),
        name="send",
    )(plan, high, low, rot)


def stay_kernel(plan_ref, high_ref, low_ref, rot_ref, kept_high, kept_low, sums_ref, acc):
    acc[...] = jnp.zeros_like(acc)
    for r, count in pieces(high_ref.shape[1]):
        for pair in range(2):
            x = stacked(high_ref, low_ref, plan_ref, 0, pair, r, count)
            new = jnp.dot(x, rot_ref[pair, :, :BW], preferred_element_type=jnp.float32)
            h, l = split(new)
            kept_high[pair, r : r + count, :] = h
            kept_low[pair, r : r + count, :] = l
            add_squares(acc, pair, new)
    for row in range(4):
        sums_ref[row : row + 1, :] = jnp.sum(acc[row], axis=0, keepdims=True)
    sums_ref[4:8] = jnp.zeros((4, 128), jnp.float32)


def stay(plan, high, low, rot):
    rows = high.shape[1]
    *kept, sums = pl.pallas_call(
        stay_kernel,
        in_specs=[in_smem] + [in_vmem] * 3,
        out_specs=[in_vmem] * 3,
        out_shape=[bf16(2, rows, BW)] * 2 + [f32(8, 128)],
        scratch_shapes=[pltpu.VMEM((4, 8, 128), jnp.float32)],
        compiler_params=params(),
        cost_estimate=cost(1 << 10, 1 << 10),
        name="stay",
    )(plan, high, low, rot)
    return kept, sums


def gram_kernel(total_rows, kept_high, kept_low, up, down, *refs):
    outs, gram_acc = refs[:4], refs[4]
    for r, count in pieces(up.shape[0]):
        here = slice(r, r + count)
        for pair, sent in enumerate((up, down)):
            h, l = split(sent[here, :])
            gram = half_gram(
                jnp.concatenate([kept_high[pair, here, :], h], axis=1),
                jnp.concatenate([kept_low[pair, here, :], l], axis=1),
            )
            gram_acc[pair] = gram + gram_acc[pair] if r else gram
    for pair in range(2):
        cut_gram(total_rows, pair, gram_acc, *outs[2 * pair : 2 * pair + 2])


def gram(total_rows, kept, up, down):
    outs = pl.pallas_call(
        functools.partial(gram_kernel, total_rows),
        in_specs=[in_vmem] * 4,
        out_specs=[in_vmem] * 4,
        out_shape=[f32(2, 128, 2 * BW)] * 4,
        scratch_shapes=[pltpu.VMEM((2, 2 * BW, 2 * BW), jnp.float32)],
        compiler_params=params(),
        cost_estimate=cost(1 << 10, 1 << 10),
        name="gram",
    )(*kept, up, down)
    return outs[:2], outs[2:]


def send_again_kernel(plan_ref, kept_high, kept_low, up_in, down_in, rot_ref, _,
                      out_up, out_down, high_ref, low_ref):
    for slot in range(2):
        high_ref[slot] = kept_high[slot]
        low_ref[slot] = kept_low[slot]
    high_ref[2], low_ref[2] = split(up_in[...])
    high_ref[3], low_ref[3] = split(down_in[...])
    for r, count in pieces(up_in.shape[0]):
        for pair, sent in enumerate((out_up, out_down)):
            x = stacked(high_ref, low_ref, plan_ref, 1, pair, r, count)
            sent[r : r + count, :] = jnp.dot(
                x, rot_ref[pair, :, BW:], preferred_element_type=jnp.float32
            )


def send_again(plan, kept, up, down, rot, after):
    rows = up.shape[0]
    return pl.pallas_call(
        send_again_kernel,
        in_specs=[in_smem] + [in_vmem] * 5 + [anywhere],
        out_specs=[in_vmem] * 4,
        out_shape=[f32(rows, BW)] * 2 + [bf16(4, rows, BW)] * 2,
        compiler_params=params(),
        cost_estimate=cost(1 << 10, 1 << 10),
        name="send_again",
    )(plan, *kept, up, down, rot, after)


def stay_again_kernel(total_rows, plan_ref, high_ref, low_ref, rot_ref, up, down, result, *refs):
    outs, (gram_acc, kept_ref, sem) = refs[:4], refs[4:]
    copies = []
    for k, (r, count) in enumerate(pieces(up.shape[0])):
        here = slice(r, r + count)
        for pair, sent in enumerate((up, down)):
            x = stacked(high_ref, low_ref, plan_ref, 1, pair, r, count)
            new = jnp.dot(x, rot_ref[pair, :, :BW], preferred_element_type=jnp.float32)
            kept_ref[here, pair * BW : (pair + 1) * BW] = new
            h, l = split(new)
            sent_h, sent_l = split(sent[here, :])
            gram = half_gram(
                jnp.concatenate([h, sent_h], axis=1), jnp.concatenate([l, sent_l], axis=1)
            )
            gram_acc[pair] = gram + gram_acc[pair] if r else gram
        copies.append(
            pltpu.make_async_copy(
                kept_ref.at[pl.ds(r, count), :],
                result.at[pl.ds(r, count), pl.ds(0, 2 * BW)],
                sem.at[k],
            )
        )
        copies[-1].start()
    for pair in range(2):
        cut_gram(total_rows, pair, gram_acc, *outs[2 * pair : 2 * pair + 2])
    for copy in copies:
        copy.wait()


def stay_again(total_rows, plan, high, low, rot, up, down):
    rows = up.shape[0]
    result, *outs = pl.pallas_call(
        functools.partial(stay_again_kernel, total_rows),
        in_specs=[in_smem] + [in_vmem] * 5,
        out_specs=[in_hbm] + [in_vmem] * 4,
        out_shape=[f32(rows, 4 * BW)] + [f32(2, 128, 2 * BW)] * 4,
        scratch_shapes=[
            pltpu.VMEM((2, 2 * BW, 2 * BW), jnp.float32),
            pltpu.VMEM((rows, 2 * BW), jnp.float32),
            pltpu.SemaphoreType.DMA((len(pieces(rows)),)),
        ],
        compiler_params=params(),
        cost_estimate=cost(1 << 10, 1 << 10),
        name="stay_again",
    )(plan, high, low, rot, up, down)
    return result, (outs[:2], outs[2:])


def mix_kernel(own, before, after, out):
    out[0:4] = own[0:4]
    for k, ref in enumerate((before, after)):
        for half in range(2):
            row = 4 + 2 * k + half
            lanes = slice(half * 128, (half + 1) * 128)
            out[row : row + 1, :] = jnp.sum(ref[:, lanes], axis=0, keepdims=True)


def mix(own, before, after):
    return pl.pallas_call(
        mix_kernel,
        in_specs=[in_vmem] * 3,
        out_specs=in_vmem,
        out_shape=f32(8, 128),
        compiler_params=params(),
        cost_estimate=cost(1 << 10, 1 << 10),
        name="mix",
    )(own, before, after)


def add_kernel(mine, got, *refs):
    keep_ref, send_ref = refs[-2:]
    keep_ref[...] = mine[0] + got[0]
    send_ref[...] = mine[1] + got[1]


def add_first(mine, got, after):
    return pl.pallas_call(
        add_kernel,
        in_specs=[in_vmem] * 2 + [anywhere] * len(after),
        out_specs=[in_vmem] * 2,
        out_shape=[f32(128, 2 * BW)] * 2,
        compiler_params=params(),
        cost_estimate=cost(1 << 10, 1 << 10),
        name="add",
    )(mine, got, *after)


def halve_kernel(mine0, got0, mine1, got1, keep_ref, send_ref):
    bit = lax.axis_index("frame") % 2
    for pair, (mine, got) in enumerate(((mine0, got0), (mine1, got1))):
        for ref, chosen in ((keep_ref, bit), (send_ref, 1 - bit)):
            rows = pl.ds(pl.multiple_of(64 * chosen, 64), 64)
            ref[pair] = mine[rows, :] + got[rows, :]


def halve(mine0, got0, mine1, got1):
    return pl.pallas_call(
        halve_kernel,
        in_specs=[in_vmem] * 4,
        out_specs=[in_vmem] * 2,
        out_shape=[f32(2, 64, 2 * BW)] * 2,
        compiler_params=params(),
        cost_estimate=cost(1 << 10, 1 << 10),
        name="halve",
    )(mine0, got0, mine1, got1)


def fill_kernel(_, up, down, out, done, sem):
    copies = [
        pltpu.make_async_copy(ref, out.at[:, pl.ds((2 + k) * BW, BW)], sem.at[k])
        for k, ref in enumerate((up, down))
    ]
    for copy in copies:
        copy.start()
    done[...] = jnp.zeros_like(done)
    for copy in copies:
        copy.wait()


def fill(out, up, down):
    return pl.pallas_call(
        fill_kernel,
        in_specs=[in_hbm, in_vmem, in_vmem],
        out_specs=[in_hbm, in_vmem],
        out_shape=[jax.ShapeDtypeStruct(out.shape, out.dtype), f32(8, 128)],
        input_output_aliases={0: 0},
        scratch_shapes=[pltpu.SemaphoreType.DMA((2,))],
        compiler_params=params(),
        cost_estimate=cost(1 << 10, 1 << 10),
        name="fill",
    )(out, up, down)


def finish_kernel(*refs):
    out = refs[-1]
    for step in range(STEPS):
        mine, got = refs[2 * step], refs[2 * step + 1]
        for pair in range(2):
            out[step, :, pair, :] = mine[pair] + got[pair]


def finish(pieces, after):
    args = [array for piece in pieces for array in piece]
    return pl.pallas_call(
        finish_kernel,
        in_specs=[in_vmem] * len(args) + [anywhere],
        out_specs=in_vmem,
        out_shape=f32(STEPS, 64, 2, 2 * BW),
        compiler_params=params(),
        cost_estimate=cost(1 << 10, 1 << 10),
        name="finish",
    )(*args, after)


def shift(x, by):
    size = lax.axis_size("pair")
    return lax.ppermute(x, "pair", [(i, (i + by) % size) for i in range(size)])


def swap(x, bit):
    size = lax.axis_size("frame")
    return lax.ppermute(x, "frame", [(i, i ^ bit) for i in range(size)])


def shift_aside(x, by):
    frames, holders = lax.axis_size("frame"), lax.axis_size("pair")
    pairs = [
        (f * holders + h, (f ^ 6) * holders + (h + by) % holders)
        for f in range(frames)
        for h in range(holders)
    ]
    return lax.ppermute(x, ("frame", "pair"), pairs)


def all_sum(x, across):
    x = (x + swap(x, 2)) + (swap(x, 6) + swap(x, 4))
    return x, swap(x, across)


NEAR = ((2, 6), (6, 2))


def begin_sum(halves, after=()):
    return [
        add_first(mine, swap(other, NEAR[pair][0]), after)
        for pair, (mine, other) in enumerate(halves)
    ]


def end_sum(begun):
    args = [(kept, swap(sent, NEAR[pair][1])) for pair, (kept, sent) in enumerate(begun)]
    mine, other = halve(*args[0], *args[1])
    return mine, swap(other, 1)


def local(columns, rotations, plan):
    total_rows = columns.shape[0] * lax.axis_size("frame")
    high, low, sums = first(columns)
    rot = scaled(total_rows, 0, all_sum(sums, 1), rotations, plan)
    up, down, up_sums, down_sums = send(plan, high, low, rot)
    moved = shift(up, 1), shift(down, -1)
    kept, own = stay(plan, high, low, rot)
    mixed = mix(own, shift_aside(up_sums, 1), shift_aside(down_sums, -1))
    halves = gram(total_rows, kept, up, down)
    rot = scaled(total_rows, 1, all_sum(mixed, 7), rotations, plan, (halves[0][0],))
    up, down, high, low = send_again(plan, kept, *moved, rot, halves[0][0])
    moved = shift(up, 1), shift(down, -1)
    result, halves_again = stay_again(total_rows, plan, high, low, rot, up, down)
    first_grams = end_sum(begin_sum(halves, (halves_again[0][0],)))
    last_grams = end_sum(begin_sum(halves_again))
    result, done = fill(result, *moved)
    return result, finish((first_grams, last_grams), done)


def solution(mesh):
    in_specs = (P("frame", "pair"), P(None, "pair", None, None), P(None, "pair", None))
    out_specs = (P("frame", "pair"), P(None, "frame", "pair", None))
    return jax.shard_map(local, mesh=mesh, in_specs=in_specs, out_specs=out_specs, check_vma=False)
```

```python
import functools

import jax
import jax.numpy as jnp
from jax import lax
from jax.experimental import pallas as pl
from jax.experimental.pallas import tpu as pltpu
from jax.sharding import PartitionSpec as P

BW = 256
STEPS = 2
READ = 256
CHUNK = 512
LONG = 512
VMEM = 16 * 1024 * 1024

epsilon = 1e-06

in_vmem = pl.BlockSpec(memory_space=pltpu.VMEM)
in_smem = pl.BlockSpec(memory_space=pltpu.SMEM)
in_hbm = pl.BlockSpec(memory_space=pltpu.HBM)
anywhere = pl.BlockSpec(memory_space=pl.ANY)


def f32(*shape):
    return jax.ShapeDtypeStruct(shape, jnp.float32)


def bf16(*shape):
    return jax.ShapeDtypeStruct(shape, jnp.bfloat16)


def params(limit=VMEM):
    return pltpu.CompilerParams(vmem_limit_bytes=limit)


def cost(flops, nbytes):
    return pl.CostEstimate(flops=flops, bytes_accessed=nbytes, transcendentals=0)


def split(x):
    high = x.astype(jnp.bfloat16)
    low = (x - high.astype(jnp.float32)).astype(jnp.bfloat16)
    return high, low


def add_squares(acc, slot, x):
    rows, cols = x.shape
    for half in range(cols // 128):
        piece = x[:, half * 128 : (half + 1) * 128]
        acc[2 * slot + half] += jnp.sum((piece * piece).reshape(rows // 8, 8, 128), axis=0)


def put_sums(sums_ref, acc):
    for row in range(8):
        sums_ref[row : row + 1, :] = jnp.sum(acc[row], axis=0, keepdims=True)


def first_kernel(x_ref, high_ref, low_ref, sums_ref, x, sem, acc):
    rows = x_ref.shape[0]
    copies = []
    for i in range(rows // READ):
        here = pl.ds(i * READ, READ)
        copies.append(pltpu.make_async_copy(x_ref.at[here, :], x.at[here, :], sem.at[i]))
    for copy in copies:
        copy.start()
    acc[...] = jnp.zeros_like(acc)
    for i, copy in enumerate(copies):
        here = slice(i * READ, (i + 1) * READ)
        copy.wait()
        for slot in range(4):
            piece = x[here, slot * BW : (slot + 1) * BW]
            add_squares(acc, slot, piece)
            high_ref[slot, here, :], low_ref[slot, here, :] = split(piece)
    put_sums(sums_ref, acc)


def first(columns):
    rows, cols = columns.shape
    return pl.pallas_call(
        first_kernel,
        in_specs=[in_hbm],
        out_specs=[in_vmem] * 3,
        out_shape=[bf16(4, rows, BW), bf16(4, rows, BW), f32(8, 128)],
        scratch_shapes=[
            pltpu.VMEM((rows, cols), jnp.float32),
            pltpu.SemaphoreType.DMA((rows // READ,)),
            pltpu.VMEM((8, 8, 128), jnp.float32),
        ],
        compiler_params=params(44 * 1024 * 1024),
        cost_estimate=cost(1 << 10, 1 << 10),
        name="first",
    )(columns)


def scale_kernel(total_rows, step, plan_ref, here_ref, there_ref, rot_ref, *refs):
    out_ref, scratch = refs[-2:]
    sums = here_ref[...] + there_ref[...]
    scratch[...] = jnp.sqrt(jnp.float32(total_rows)) * lax.rsqrt(sums + epsilon)
    for k in range(4):
        pair, half = k // 2, k % 2
        for part in range(2):
            row = scratch[pl.ds(2 * plan_ref[step, 0, k] + part, 1), :]
            column = jnp.broadcast_to(row, (128, 128)).T
            top = half * BW + part * 128
            for c in range(4):
                lanes = slice(c * 128, (c + 1) * 128)
                h, l = split(rot_ref[step, pair, top : top + 128, lanes] * column)
                out_ref[pair, top : top + 128, lanes] = h
                out_ref[pair, 2 * BW + top : 2 * BW + top + 128, lanes] = h
                out_ref[pair, 4 * BW + top : 4 * BW + top + 128, lanes] = l


def scaled(total_rows, step, sums, rotations, plan, after=()):
    return pl.pallas_call(
        functools.partial(scale_kernel, total_rows, step),
        in_specs=[in_smem] + [in_vmem] * 3 + [anywhere] * len(after),
        out_specs=in_vmem,
        out_shape=bf16(2, 6 * BW, 2 * BW),
        scratch_shapes=[pltpu.VMEM((8, 128), jnp.float32)],
        compiler_params=params(),
        cost_estimate=cost(1 << 10, 1 << 10),
        name="scale",
    )(plan, *sums, rotations, *after)


def pieces(rows, longest=CHUNK):
    count = -(-rows // longest)
    return [(k * (rows // count), rows // count) for k in range(count)]


def stacked(high_ref, low_ref, plan_ref, step, pair, row, count):
    slots = [plan_ref[step, 0, 2 * pair + k] for k in range(2)]
    h = [high_ref[slot, row : row + count, :] for slot in slots]
    l = [low_ref[slot, row : row + count, :] for slot in slots]
    return jnp.concatenate(h + l + h, axis=1)


def half_gram(nh, nl):
    turned = nh.T
    return jnp.dot(
        jnp.concatenate([turned, turned], axis=1),
        jnp.concatenate([nh * jnp.bfloat16(0.5), nl], axis=0),
        preferred_element_type=jnp.float32,
    )


def cut_gram(total_rows, pair, gram_acc, mine, other):
    half = gram_acc[pair]
    gram_acc[pair] = (half + half.T) * jnp.float32(1.0 / total_rows)
    x = lax.axis_index("frame") // 2
    near = x + 1 - 2 * (x % 2)
    blocks = (((x, 3 - x), (near, 3 - near)), ((x, near), (3 - x, 3 - near)))[pair]
    for ref, rows in zip((mine, other), blocks):
        for k in range(2):
            row = pl.multiple_of(128 * rows[k], 128)
            ref[k] = gram_acc[pair, pl.ds(row, 128), :]


def send_kernel(plan_ref, high_ref, low_ref, rot_ref, up, down, up_sums, down_sums, acc):
    acc[...] = jnp.zeros_like(acc)
    for r, count in pieces(up.shape[0]):
        for pair, sent in enumerate((up, down)):
            x = stacked(high_ref, low_ref, plan_ref, 0, pair, r, count)
            new = jnp.dot(x, rot_ref[pair, :, BW:], preferred_element_type=jnp.float32)
            sent[r : r + count, :] = new
            add_squares(acc, pair, new)
    for pair, sums in enumerate((up_sums, down_sums)):
        for half in range(2):
            sums[:, half * 128 : (half + 1) * 128] = acc[2 * pair + half]


def send(plan, high, low, rot):
    rows = high.shape[1]
    return pl.pallas_call(
        send_kernel,
        in_specs=[in_smem] + [in_vmem] * 3,
        out_specs=[in_vmem] * 4,
        out_shape=[f32(rows, BW)] * 2 + [f32(8, BW)] * 2,
        scratch_shapes=[pltpu.VMEM((4, 8, 128), jnp.float32)],
        compiler_params=params(),
        cost_estimate=cost(1 << 10, 1 << 10),
        name="send",
    )(plan, high, low, rot)


def stay_kernel(plan_ref, high_ref, low_ref, rot_ref, kept_high, kept_low, sums_ref, acc):
    acc[...] = jnp.zeros_like(acc)
    for r, count in pieces(high_ref.shape[1]):
        for pair in range(2):
            x = stacked(high_ref, low_ref, plan_ref, 0, pair, r, count)
            new = jnp.dot(x, rot_ref[pair, :, :BW], preferred_element_type=jnp.float32)
            h, l = split(new)
            kept_high[pair, r : r + count, :] = h
            kept_low[pair, r : r + count, :] = l
            add_squares(acc, pair, new)
    for row in range(4):
        sums_ref[row : row + 1, :] = jnp.sum(acc[row], axis=0, keepdims=True)
    sums_ref[4:8] = jnp.zeros((4, 128), jnp.float32)


def stay(plan, high, low, rot):
    rows = high.shape[1]
    *kept, sums = pl.pallas_call(
        stay_kernel,
        in_specs=[in_smem] + [in_vmem] * 3,
        out_specs=[in_vmem] * 3,
        out_shape=[bf16(2, rows, BW)] * 2 + [f32(8, 128)],
        scratch_shapes=[pltpu.VMEM((4, 8, 128), jnp.float32)],
        compiler_params=params(),
        cost_estimate=cost(1 << 10, 1 << 10),
        name="stay",
    )(plan, high, low, rot)
    return kept, sums


def gram_kernel(total_rows, kept_high, kept_low, up, down, *refs):
    outs, gram_acc = refs[:4], refs[4]
    for r, count in pieces(up.shape[0]):
        here = slice(r, r + count)
        for pair, sent in enumerate((up, down)):
            h, l = split(sent[here, :])
            gram = half_gram(
                jnp.concatenate([kept_high[pair, here, :], h], axis=1),
                jnp.concatenate([kept_low[pair, here, :], l], axis=1),
            )
            gram_acc[pair] = gram + gram_acc[pair] if r else gram
    for pair in range(2):
        cut_gram(total_rows, pair, gram_acc, *outs[2 * pair : 2 * pair + 2])


def gram(total_rows, kept, up, down):
    outs = pl.pallas_call(
        functools.partial(gram_kernel, total_rows),
        in_specs=[in_vmem] * 4,
        out_specs=[in_vmem] * 4,
        out_shape=[f32(2, 128, 2 * BW)] * 4,
        scratch_shapes=[pltpu.VMEM((2, 2 * BW, 2 * BW), jnp.float32)],
        compiler_params=params(),
        cost_estimate=cost(1 << 10, 1 << 10),
        name="gram",
    )(*kept, up, down)
    return outs[:2], outs[2:]


def send_again_kernel(plan_ref, kept_high, kept_low, up_in, down_in, rot_ref, _,
                      out_up, out_down, high_ref, low_ref):
    for slot in range(2):
        high_ref[slot] = kept_high[slot]
        low_ref[slot] = kept_low[slot]
    high_ref[2], low_ref[2] = split(up_in[...])
    high_ref[3], low_ref[3] = split(down_in[...])
    for r, count in pieces(up_in.shape[0]):
        for pair, sent in enumerate((out_up, out_down)):
            x = stacked(high_ref, low_ref, plan_ref, 1, pair, r, count)
            sent[r : r + count, :] = jnp.dot(
                x, rot_ref[pair, :, BW:], preferred_element_type=jnp.float32
            )


def send_again(plan, kept, up, down, rot, after):
    rows = up.shape[0]
    return pl.pallas_call(
        send_again_kernel,
        in_specs=[in_smem] + [in_vmem] * 5 + [anywhere],
        out_specs=[in_vmem] * 4,
        out_shape=[f32(rows, BW)] * 2 + [bf16(4, rows, BW)] * 2,
        compiler_params=params(),
        cost_estimate=cost(1 << 10, 1 << 10),
        name="send_again",
    )(plan, *kept, up, down, rot, after)


def stay_again_kernel(total_rows, plan_ref, high_ref, low_ref, rot_ref, up, down, result, *refs):
    outs, (gram_acc, kept_ref, sem) = refs[:4], refs[4:]
    copies = []
    for k, (r, count) in enumerate(pieces(up.shape[0], LONG)):
        here = slice(r, r + count)
        for pair, sent in enumerate((up, down)):
            x = stacked(high_ref, low_ref, plan_ref, 1, pair, r, count)
            new = jnp.dot(x, rot_ref[pair, :, :BW], preferred_element_type=jnp.float32)
            kept_ref[here, pair * BW : (pair + 1) * BW] = new
            h, l = split(new)
            sent_h, sent_l = split(sent[here, :])
            gram = half_gram(
                jnp.concatenate([h, sent_h], axis=1), jnp.concatenate([l, sent_l], axis=1)
            )
            gram_acc[pair] = gram + gram_acc[pair] if r else gram
        copies.append(
            pltpu.make_async_copy(
                kept_ref.at[pl.ds(r, count), :],
                result.at[pl.ds(r, count), pl.ds(0, 2 * BW)],
                sem.at[k],
            )
        )
        copies[-1].start()
    for pair in range(2):
        cut_gram(total_rows, pair, gram_acc, *outs[2 * pair : 2 * pair + 2])
    for copy in copies:
        copy.wait()


def stay_again(total_rows, plan, high, low, rot, up, down):
    rows = up.shape[0]
    result, *outs = pl.pallas_call(
        functools.partial(stay_again_kernel, total_rows),
        in_specs=[in_smem] + [in_vmem] * 5,
        out_specs=[in_hbm] + [in_vmem] * 4,
        out_shape=[f32(rows, 4 * BW)] + [f32(2, 128, 2 * BW)] * 4,
        scratch_shapes=[
            pltpu.VMEM((2, 2 * BW, 2 * BW), jnp.float32),
            pltpu.VMEM((rows, 2 * BW), jnp.float32),
            pltpu.SemaphoreType.DMA((len(pieces(rows, LONG)),)),
        ],
        compiler_params=params(),
        cost_estimate=cost(1 << 10, 1 << 10),
        name="stay_again",
    )(plan, high, low, rot, up, down)
    return result, (outs[:2], outs[2:])


def mix_kernel(own, before, after, out):
    out[0:4] = own[0:4]
    for k, ref in enumerate((before, after)):
        for half in range(2):
            row = 4 + 2 * k + half
            lanes = slice(half * 128, (half + 1) * 128)
            out[row : row + 1, :] = jnp.sum(ref[:, lanes], axis=0, keepdims=True)


def mix(own, before, after):
    return pl.pallas_call(
        mix_kernel,
        in_specs=[in_vmem] * 3,
        out_specs=in_vmem,
        out_shape=f32(8, 128),
        compiler_params=params(),
        cost_estimate=cost(1 << 10, 1 << 10),
        name="mix",
    )(own, before, after)


def add_kernel(mine, got, *refs):
    keep_ref, send_ref = refs[-2:]
    keep_ref[...] = mine[0] + got[0]
    send_ref[...] = mine[1] + got[1]


def add_first(mine, got, after):
    return pl.pallas_call(
        add_kernel,
        in_specs=[in_vmem] * 2 + [anywhere] * len(after),
        out_specs=[in_vmem] * 2,
        out_shape=[f32(128, 2 * BW)] * 2,
        compiler_params=params(),
        cost_estimate=cost(1 << 10, 1 << 10),
        name="add",
    )(mine, got, *after)


def halve_kernel(mine0, got0, mine1, got1, keep_ref, send_ref):
    bit = lax.axis_index("frame") % 2
    for pair, (mine, got) in enumerate(((mine0, got0), (mine1, got1))):
        for ref, chosen in ((keep_ref, bit), (send_ref, 1 - bit)):
            rows = pl.ds(pl.multiple_of(64 * chosen, 64), 64)
            ref[pair] = mine[rows, :] + got[rows, :]


def halve(mine0, got0, mine1, got1):
    return pl.pallas_call(
        halve_kernel,
        in_specs=[in_vmem] * 4,
        out_specs=[in_vmem] * 2,
        out_shape=[f32(2, 64, 2 * BW)] * 2,
        compiler_params=params(),
        cost_estimate=cost(1 << 10, 1 << 10),
        name="halve",
    )(mine0, got0, mine1, got1)


def halve_early_kernel(mine0, got0, mine1, got1, _, keep_ref, send_ref):
    bit = lax.axis_index("frame") % 2
    for pair, (mine, got) in enumerate(((mine0, got0), (mine1, got1))):
        for ref, chosen in ((keep_ref, bit), (send_ref, 1 - bit)):
            rows = pl.ds(pl.multiple_of(64 * chosen, 64), 64)
            ref[pair] = mine[:, rows, :] + got[:, rows, :]


def halve_early(args, after):
    return pl.pallas_call(
        halve_early_kernel,
        in_specs=[in_vmem] * 4 + [anywhere],
        out_specs=[in_vmem] * 2,
        out_shape=[f32(2, 2, 64, 2 * BW)] * 2,
        compiler_params=params(),
        cost_estimate=cost(1 << 10, 1 << 10),
        name="halve_early",
    )(*args, after)


def pass_on_kernel(mine, got, keep_ref, send0, send1):
    for pair, sent in enumerate((send0, send1)):
        keep_ref[pair] = mine[pair, 0] + got[pair, 0]
        sent[...] = mine[pair, 1] + got[pair, 1]


def pass_on(mine, got):
    return pl.pallas_call(
        pass_on_kernel,
        in_specs=[in_vmem] * 2,
        out_specs=[in_vmem] * 3,
        out_shape=[f32(2, 64, 2 * BW), f32(64, 2 * BW), f32(64, 2 * BW)],
        compiler_params=params(),
        cost_estimate=cost(1 << 10, 1 << 10),
        name="pass_on",
    )(mine, got)


def fill_kernel(_, up, down, out, done, sem):
    copies = [
        pltpu.make_async_copy(ref, out.at[:, pl.ds((2 + k) * BW, BW)], sem.at[k])
        for k, ref in enumerate((up, down))
    ]
    for copy in copies:
        copy.start()
    done[...] = jnp.zeros_like(done)
    for copy in copies:
        copy.wait()


def fill(out, up, down):
    return pl.pallas_call(
        fill_kernel,
        in_specs=[in_hbm, in_vmem, in_vmem],
        out_specs=[in_hbm, in_vmem],
        out_shape=[jax.ShapeDtypeStruct(out.shape, out.dtype), f32(8, 128)],
        input_output_aliases={0: 0},
        scratch_shapes=[pltpu.SemaphoreType.DMA((2,))],
        compiler_params=params(),
        cost_estimate=cost(1 << 10, 1 << 10),
        name="fill",
    )(out, up, down)


def finish_kernel(first_mine, first_got0, first_got1, last_mine, last_got, _, out):
    for pair, got in enumerate((first_got0, first_got1)):
        out[0, :, pair, :] = first_mine[pair] + got[...]
        out[1, :, pair, :] = last_mine[pair] + last_got[pair]


def finish(first_grams, last_grams, after):
    return pl.pallas_call(
        finish_kernel,
        in_specs=[in_vmem] * 5 + [anywhere],
        out_specs=in_vmem,
        out_shape=f32(STEPS, 64, 2, 2 * BW),
        compiler_params=params(),
        cost_estimate=cost(1 << 10, 1 << 10),
        name="finish",
    )(*first_grams, *last_grams, after)


def shift(x, by):
    size = lax.axis_size("pair")
    return lax.ppermute(x, "pair", [(i, (i + by) % size) for i in range(size)])


def swap(x, bit):
    size = lax.axis_size("frame")
    return lax.ppermute(x, "frame", [(i, i ^ bit) for i in range(size)])


def shift_aside(x, by):
    frames, holders = lax.axis_size("frame"), lax.axis_size("pair")
    pairs = [
        (f * holders + h, (f ^ 6) * holders + (h + by) % holders)
        for f in range(frames)
        for h in range(holders)
    ]
    return lax.ppermute(x, ("frame", "pair"), pairs)


def all_sum(x, across):
    x = (x + swap(x, 2)) + (swap(x, 6) + swap(x, 4))
    return x, swap(x, across)


NEAR = ((2, 6), (6, 2))


def last_sum(halves):
    args = []
    for (mine, other), (here, there) in zip(halves, NEAR):
        kept, sent = add_first(mine, swap(other, here), ())
        args += [kept, swap(sent, there)]
    mine, other = halve(*args)
    return mine, swap(other, 1)


def first_sum(halves, after):
    args = []
    for (mine, other), (here, _) in zip(halves, NEAR):
        args += [mine, swap(other, here)]
    mine, other = halve_early(args, after)
    mine, *sent = pass_on(mine, swap(other, 1))
    return mine, swap(sent[0], NEAR[0][1]), swap(sent[1], NEAR[1][1])


def local(columns, rotations, plan):
    total_rows = columns.shape[0] * lax.axis_size("frame")
    high, low, sums = first(columns)
    rot = scaled(total_rows, 0, all_sum(sums, 1), rotations, plan)
    up, down, up_sums, down_sums = send(plan, high, low, rot)
    moved = shift(up, 1), shift(down, -1)
    kept, own = stay(plan, high, low, rot)
    mixed = mix(own, shift_aside(up_sums, 1), shift_aside(down_sums, -1))
    halves = gram(total_rows, kept, up, down)
    rot = scaled(total_rows, 1, all_sum(mixed, 7), rotations, plan, (halves[0][0],))
    up, down, high, low = send_again(plan, kept, *moved, rot, halves[0][0])
    moved = shift(up, 1), shift(down, -1)
    result, halves_again = stay_again(total_rows, plan, high, low, rot, up, down)
    first_grams = first_sum(halves, halves_again[0][0])
    last_grams = last_sum(halves_again)
    result, done = fill(result, *moved)
    return result, finish(first_grams, last_grams, done)


def solution(mesh):
    in_specs = (P("frame", "pair"), P(None, "pair", None, None), P(None, "pair", None))
    out_specs = (P("frame", "pair"), P(None, "frame", "pair", None))
    return jax.shard_map(local, mesh=mesh, in_specs=in_specs, out_specs=out_specs, check_vma=False)
```

```python
import functools

import jax
import jax.numpy as jnp
from jax import lax
from jax.experimental import pallas as pl
from jax.experimental.pallas import tpu as pltpu
from jax.sharding import PartitionSpec as P

BW = 256
STEPS = 2
READ = 256
CHUNK = 512
LONG = 512
VMEM = 16 * 1024 * 1024

epsilon = 1e-06

in_vmem = pl.BlockSpec(memory_space=pltpu.VMEM)
in_smem = pl.BlockSpec(memory_space=pltpu.SMEM)
in_hbm = pl.BlockSpec(memory_space=pltpu.HBM)
anywhere = pl.BlockSpec(memory_space=pl.ANY)


def f32(*shape):
    return jax.ShapeDtypeStruct(shape, jnp.float32)


def bf16(*shape):
    return jax.ShapeDtypeStruct(shape, jnp.bfloat16)


def params(limit=VMEM):
    return pltpu.CompilerParams(vmem_limit_bytes=limit)


def cost(flops, nbytes):
    return pl.CostEstimate(flops=flops, bytes_accessed=nbytes, transcendentals=0)


def split(x):
    high = x.astype(jnp.bfloat16)
    low = (x - high.astype(jnp.float32)).astype(jnp.bfloat16)
    return high, low


def add_squares(acc, slot, x):
    rows, cols = x.shape
    for half in range(cols // 128):
        piece = x[:, half * 128 : (half + 1) * 128]
        acc[2 * slot + half] += jnp.sum((piece * piece).reshape(rows // 8, 8, 128), axis=0)


def put_sums(sums_ref, acc):
    for row in range(8):
        sums_ref[row : row + 1, :] = jnp.sum(acc[row], axis=0, keepdims=True)


def first_kernel(x_ref, high_ref, low_ref, sums_ref, x, sem, acc):
    rows = x_ref.shape[0]
    copies = []
    for i in range(rows // READ):
        here = pl.ds(i * READ, READ)
        copies.append(pltpu.make_async_copy(x_ref.at[here, :], x.at[here, :], sem.at[i]))
    for copy in copies:
        copy.start()
    acc[...] = jnp.zeros_like(acc)
    for i, copy in enumerate(copies):
        here = slice(i * READ, (i + 1) * READ)
        copy.wait()
        for slot in range(4):
            piece = x[here, slot * BW : (slot + 1) * BW]
            add_squares(acc, slot, piece)
            high_ref[slot, here, :], low_ref[slot, here, :] = split(piece)
    put_sums(sums_ref, acc)


def first(columns):
    rows, cols = columns.shape
    return pl.pallas_call(
        first_kernel,
        in_specs=[in_hbm],
        out_specs=[in_vmem] * 3,
        out_shape=[bf16(4, rows, BW), bf16(4, rows, BW), f32(8, 128)],
        scratch_shapes=[
            pltpu.VMEM((rows, cols), jnp.float32),
            pltpu.SemaphoreType.DMA((rows // READ,)),
            pltpu.VMEM((8, 8, 128), jnp.float32),
        ],
        compiler_params=params(44 * 1024 * 1024),
        cost_estimate=cost(1 << 10, 1 << 10),
        name="first",
    )(columns)


def scale_kernel(total_rows, step, plan_ref, here_ref, there_ref, rot_ref, *refs):
    out_ref, scratch = refs[-2:]
    sums = here_ref[...] + there_ref[...]
    scratch[...] = jnp.sqrt(jnp.float32(total_rows)) * lax.rsqrt(sums + epsilon)
    for k in range(4):
        pair, half = k // 2, k % 2
        for part in range(2):
            row = scratch[pl.ds(2 * plan_ref[step, 0, k] + part, 1), :]
            column = jnp.broadcast_to(row, (128, 128)).T
            top = half * BW + part * 128
            for c in range(4):
                lanes = slice(c * 128, (c + 1) * 128)
                h, l = split(rot_ref[step, pair, top : top + 128, lanes] * column)
                out_ref[pair, top : top + 128, lanes] = h
                out_ref[pair, 2 * BW + top : 2 * BW + top + 128, lanes] = h
                out_ref[pair, 4 * BW + top : 4 * BW + top + 128, lanes] = l


def scaled(total_rows, step, sums, rotations, plan, after=()):
    return pl.pallas_call(
        functools.partial(scale_kernel, total_rows, step),
        in_specs=[in_smem] + [in_vmem] * 3 + [anywhere] * len(after),
        out_specs=in_vmem,
        out_shape=bf16(2, 6 * BW, 2 * BW),
        scratch_shapes=[pltpu.VMEM((8, 128), jnp.float32)],
        compiler_params=params(),
        cost_estimate=cost(1 << 10, 1 << 10),
        name="scale",
    )(plan, *sums, rotations, *after)


def pieces(rows, longest=CHUNK):
    count = -(-rows // longest)
    return [(k * (rows // count), rows // count) for k in range(count)]


def stacked(high_ref, low_ref, plan_ref, step, pair, row, count):
    slots = [plan_ref[step, 0, 2 * pair + k] for k in range(2)]
    h = [high_ref[slot, row : row + count, :] for slot in slots]
    l = [low_ref[slot, row : row + count, :] for slot in slots]
    return jnp.concatenate(h + l + h, axis=1)


def half_gram(nh, nl):
    turned = nh.T
    return jnp.dot(
        jnp.concatenate([turned, turned], axis=1),
        jnp.concatenate([nh * jnp.bfloat16(0.5), nl], axis=0),
        preferred_element_type=jnp.float32,
    )


def cut_gram(total_rows, pair, gram_acc, mine, other):
    half = gram_acc[pair]
    gram_acc[pair] = (half + half.T) * jnp.float32(1.0 / total_rows)
    x = lax.axis_index("frame") // 2
    near = x + 1 - 2 * (x % 2)
    blocks = (((x, 3 - x), (near, 3 - near)), ((x, near), (3 - x, 3 - near)))[pair]
    for ref, rows in zip((mine, other), blocks):
        for k in range(2):
            row = pl.multiple_of(128 * rows[k], 128)
            ref[k] = gram_acc[pair, pl.ds(row, 128), :]


def send_kernel(plan_ref, high_ref, low_ref, rot_ref, up, down, up_sums, down_sums, acc):
    acc[...] = jnp.zeros_like(acc)
    for r, count in pieces(up.shape[0]):
        for pair, sent in enumerate((up, down)):
            x = stacked(high_ref, low_ref, plan_ref, 0, pair, r, count)
            new = jnp.dot(x, rot_ref[pair, :, BW:], preferred_element_type=jnp.float32)
            sent[r : r + count, :] = new
            add_squares(acc, pair, new)
    for pair, sums in enumerate((up_sums, down_sums)):
        for half in range(2):
            sums[:, half * 128 : (half + 1) * 128] = acc[2 * pair + half]


def send(plan, high, low, rot):
    rows = high.shape[1]
    return pl.pallas_call(
        send_kernel,
        in_specs=[in_smem] + [in_vmem] * 3,
        out_specs=[in_vmem] * 4,
        out_shape=[f32(rows, BW)] * 2 + [f32(8, BW)] * 2,
        scratch_shapes=[pltpu.VMEM((4, 8, 128), jnp.float32)],
        compiler_params=params(),
        cost_estimate=cost(1 << 10, 1 << 10),
        name="send",
    )(plan, high, low, rot)


def stay_kernel(plan_ref, high_ref, low_ref, rot_ref, kept_high, kept_low, sums_ref, acc):
    acc[...] = jnp.zeros_like(acc)
    for r, count in pieces(high_ref.shape[1]):
        for pair in range(2):
            x = stacked(high_ref, low_ref, plan_ref, 0, pair, r, count)
            new = jnp.dot(x, rot_ref[pair, :, :BW], preferred_element_type=jnp.float32)
            h, l = split(new)
            kept_high[pair, r : r + count, :] = h
            kept_low[pair, r : r + count, :] = l
            add_squares(acc, pair, new)
    for row in range(4):
        sums_ref[row : row + 1, :] = jnp.sum(acc[row], axis=0, keepdims=True)
    sums_ref[4:8] = jnp.zeros((4, 128), jnp.float32)


def stay(plan, high, low, rot):
    rows = high.shape[1]
    *kept, sums = pl.pallas_call(
        stay_kernel,
        in_specs=[in_smem] + [in_vmem] * 3,
        out_specs=[in_vmem] * 3,
        out_shape=[bf16(2, rows, BW)] * 2 + [f32(8, 128)],
        scratch_shapes=[pltpu.VMEM((4, 8, 128), jnp.float32)],
        compiler_params=params(),
        cost_estimate=cost(1 << 10, 1 << 10),
        name="stay",
    )(plan, high, low, rot)
    return kept, sums


def gram_kernel(total_rows, pair, kept_high, kept_low, sent_ref, mine, other, gram_acc):
    for r, count in pieces(sent_ref.shape[0]):
        here = slice(r, r + count)
        h, l = split(sent_ref[here, :])
        gram = half_gram(
            jnp.concatenate([kept_high[pair, here, :], h], axis=1),
            jnp.concatenate([kept_low[pair, here, :], l], axis=1),
        )
        gram_acc[pair] = gram + gram_acc[pair] if r else gram
    cut_gram(total_rows, pair, gram_acc, mine, other)


def gram(total_rows, pair, kept, sent):
    return pl.pallas_call(
        functools.partial(gram_kernel, total_rows, pair),
        in_specs=[in_vmem] * 3,
        out_specs=[in_vmem] * 2,
        out_shape=[f32(2, 128, 2 * BW)] * 2,
        scratch_shapes=[pltpu.VMEM((2, 2 * BW, 2 * BW), jnp.float32)],
        compiler_params=params(),
        cost_estimate=cost(1 << 10, 1 << 10),
        name="gram",
    )(*kept, sent)


def send_again_kernel(plan_ref, kept_high, kept_low, up_in, down_in, rot_ref, _,
                      out_up, out_down, high_ref, low_ref):
    for slot in range(2):
        high_ref[slot] = kept_high[slot]
        low_ref[slot] = kept_low[slot]
    high_ref[2], low_ref[2] = split(up_in[...])
    high_ref[3], low_ref[3] = split(down_in[...])
    for r, count in pieces(up_in.shape[0]):
        for pair, sent in enumerate((out_up, out_down)):
            x = stacked(high_ref, low_ref, plan_ref, 1, pair, r, count)
            sent[r : r + count, :] = jnp.dot(
                x, rot_ref[pair, :, BW:], preferred_element_type=jnp.float32
            )


def send_again(plan, kept, up, down, rot, after):
    rows = up.shape[0]
    return pl.pallas_call(
        send_again_kernel,
        in_specs=[in_smem] + [in_vmem] * 5 + [anywhere],
        out_specs=[in_vmem] * 4,
        out_shape=[f32(rows, BW)] * 2 + [bf16(4, rows, BW)] * 2,
        compiler_params=params(),
        cost_estimate=cost(1 << 10, 1 << 10),
        name="send_again",
    )(plan, *kept, up, down, rot, after)


def stay_again_kernel(total_rows, plan_ref, high_ref, low_ref, rot_ref, up, down, result, *refs):
    outs, (gram_acc, kept_ref, sem) = refs[:4], refs[4:]
    copies = []
    for k, (r, count) in enumerate(pieces(up.shape[0], LONG)):
        here = slice(r, r + count)
        for pair, sent in enumerate((up, down)):
            x = stacked(high_ref, low_ref, plan_ref, 1, pair, r, count)
            new = jnp.dot(x, rot_ref[pair, :, :BW], preferred_element_type=jnp.float32)
            kept_ref[here, pair * BW : (pair + 1) * BW] = new
            h, l = split(new)
            sent_h, sent_l = split(sent[here, :])
            gram = half_gram(
                jnp.concatenate([h, sent_h], axis=1), jnp.concatenate([l, sent_l], axis=1)
            )
            gram_acc[pair] = gram + gram_acc[pair] if r else gram
        copies.append(
            pltpu.make_async_copy(
                kept_ref.at[pl.ds(r, count), :],
                result.at[pl.ds(r, count), pl.ds(0, 2 * BW)],
                sem.at[k],
            )
        )
        copies[-1].start()
    for pair in range(2):
        cut_gram(total_rows, pair, gram_acc, *outs[2 * pair : 2 * pair + 2])
    for copy in copies:
        copy.wait()


def stay_again(total_rows, plan, high, low, rot, up, down):
    rows = up.shape[0]
    result, *outs = pl.pallas_call(
        functools.partial(stay_again_kernel, total_rows),
        in_specs=[in_smem] + [in_vmem] * 5,
        out_specs=[in_hbm] + [in_vmem] * 4,
        out_shape=[f32(rows, 4 * BW)] + [f32(2, 128, 2 * BW)] * 4,
        scratch_shapes=[
            pltpu.VMEM((2, 2 * BW, 2 * BW), jnp.float32),
            pltpu.VMEM((rows, 2 * BW), jnp.float32),
            pltpu.SemaphoreType.DMA((len(pieces(rows, LONG)),)),
        ],
        compiler_params=params(),
        cost_estimate=cost(1 << 10, 1 << 10),
        name="stay_again",
    )(plan, high, low, rot, up, down)
    return result, (outs[:2], outs[2:])


def mix_kernel(own, before, after, out):
    out[0:4] = own[0:4]
    for k, ref in enumerate((before, after)):
        for half in range(2):
            row = 4 + 2 * k + half
            lanes = slice(half * 128, (half + 1) * 128)
            out[row : row + 1, :] = jnp.sum(ref[:, lanes], axis=0, keepdims=True)


def mix(own, before, after):
    return pl.pallas_call(
        mix_kernel,
        in_specs=[in_vmem] * 3,
        out_specs=in_vmem,
        out_shape=f32(8, 128),
        compiler_params=params(),
        cost_estimate=cost(1 << 10, 1 << 10),
        name="mix",
    )(own, before, after)


def add_kernel(mine, got, *refs):
    keep_ref, send_ref = refs[-2:]
    keep_ref[...] = mine[0] + got[0]
    send_ref[...] = mine[1] + got[1]


def add_first(mine, got, after):
    return pl.pallas_call(
        add_kernel,
        in_specs=[in_vmem] * 2 + [anywhere] * len(after),
        out_specs=[in_vmem] * 2,
        out_shape=[f32(mine.shape[1], 2 * BW)] * 2,
        compiler_params=params(),
        cost_estimate=cost(1 << 10, 1 << 10),
        name="add",
    )(mine, got, *after)


def halve_kernel(*refs):
    keep_ref, send_ref = refs[-2:]
    bit = lax.axis_index("frame") % 2
    for k in range(keep_ref.shape[0]):
        mine, got = refs[2 * k], refs[2 * k + 1]
        for ref, chosen in ((keep_ref, bit), (send_ref, 1 - bit)):
            rows = pl.ds(pl.multiple_of(64 * chosen, 64), 64)
            ref[k] = mine[rows, :] + got[rows, :]


def halve(terms):
    args = [array for term in terms for array in term]
    return pl.pallas_call(
        halve_kernel,
        in_specs=[in_vmem] * len(args),
        out_specs=[in_vmem] * 2,
        out_shape=[f32(len(terms), 64, 2 * BW)] * 2,
        compiler_params=params(),
        cost_estimate=cost(1 << 10, 1 << 10),
        name="halve",
    )(*args)


def begin_kernel(mine0, got0, mine1, got1, _, keep0, send0, keep1, send1):
    bit = lax.axis_index("frame") % 2
    for ref, chosen in ((keep0, bit), (send0, 1 - bit)):
        rows = pl.ds(pl.multiple_of(64 * chosen, 64), 64)
        ref[...] = mine0[:, rows, :] + got0[:, rows, :]
    keep1[...] = mine1[0] + got1[0]
    send1[...] = mine1[1] + got1[1]


def begin(args, after):
    return pl.pallas_call(
        begin_kernel,
        in_specs=[in_vmem] * 4 + [anywhere],
        out_specs=[in_vmem] * 4,
        out_shape=[f32(2, 64, 2 * BW)] * 2 + [f32(128, 2 * BW)] * 2,
        compiler_params=params(),
        cost_estimate=cost(1 << 10, 1 << 10),
        name="begin",
    )(*args, after)


def fill_kernel(_, up, down, out, done, sem):
    copies = [
        pltpu.make_async_copy(ref, out.at[:, pl.ds((2 + k) * BW, BW)], sem.at[k])
        for k, ref in enumerate((up, down))
    ]
    for copy in copies:
        copy.start()
    done[...] = jnp.zeros_like(done)
    for copy in copies:
        copy.wait()


def fill(out, up, down):
    return pl.pallas_call(
        fill_kernel,
        in_specs=[in_hbm, in_vmem, in_vmem],
        out_specs=[in_hbm, in_vmem],
        out_shape=[jax.ShapeDtypeStruct(out.shape, out.dtype), f32(8, 128)],
        input_output_aliases={0: 0},
        scratch_shapes=[pltpu.SemaphoreType.DMA((2,))],
        compiler_params=params(),
        cost_estimate=cost(1 << 10, 1 << 10),
        name="fill",
    )(out, up, down)


def finish_kernel(early_mine, early_got, mine, got, _, out):
    out[0, :, 0, :] = early_mine[...] + early_got[...]
    out[0, :, 1, :] = mine[2] + got[2]
    for pair in range(2):
        out[1, :, pair, :] = mine[pair] + got[pair]


def finish(early, late, after):
    return pl.pallas_call(
        finish_kernel,
        in_specs=[in_vmem] * 4 + [anywhere],
        out_specs=in_vmem,
        out_shape=f32(STEPS, 64, 2, 2 * BW),
        compiler_params=params(),
        cost_estimate=cost(1 << 10, 1 << 10),
        name="finish",
    )(*early, *late, after)


def shift(x, by):
    size = lax.axis_size("pair")
    return lax.ppermute(x, "pair", [(i, (i + by) % size) for i in range(size)])


def swap(x, bit):
    size = lax.axis_size("frame")
    return lax.ppermute(x, "frame", [(i, i ^ bit) for i in range(size)])


def shift_aside(x, by):
    frames, holders = lax.axis_size("frame"), lax.axis_size("pair")
    pairs = [
        (f * holders + h, (f ^ 6) * holders + (h + by) % holders)
        for f in range(frames)
        for h in range(holders)
    ]
    return lax.ppermute(x, ("frame", "pair"), pairs)


def add_kernel_of_four(a, b, c, d, *refs):
    refs[-1][...] = (a[...] + b[...]) + (c[...] + d[...])


def all_sum(x, across, after=()):
    x = pl.pallas_call(
        add_kernel_of_four,
        in_specs=[in_vmem] * 4 + [anywhere] * len(after),
        out_specs=in_vmem,
        out_shape=f32(8, 128),
        compiler_params=params(),
        cost_estimate=cost(1 << 10, 1 << 10),
        name="add_four",
    )(x, swap(x, 2), swap(x, 6), swap(x, 4), *after)
    return x, swap(x, across)


NEAR = ((2, 6), (6, 2))


def gram_sums(first_halves, last_halves):
    args = []
    for (mine, other), (here, _) in zip(first_halves, NEAR):
        args += [mine, swap(other, here)]
    mine, other, kept1, sent1 = begin(args, last_halves[0][0])
    kept, sent = add_first(mine, swap(other, 1), ())
    early = kept, swap(sent, NEAR[0][1])
    terms = []
    for (mine, other), (here, there) in zip(last_halves, NEAR):
        kept, sent = add_first(mine, swap(other, here), ())
        terms.append((kept, swap(sent, there)))
    terms.append((kept1, swap(sent1, NEAR[1][1])))
    mine, other = halve(terms)
    return early, (mine, swap(other, 1))


def local(columns, rotations, plan):
    total_rows = columns.shape[0] * lax.axis_size("frame")
    high, low, sums = first(columns)
    rot = scaled(total_rows, 0, all_sum(sums, 1), rotations, plan)
    up, down, up_sums, down_sums = send(plan, high, low, rot)
    moved = shift(up, 1), shift(down, -1)
    kept, own = stay(plan, high, low, rot)
    mixed = mix(own, shift_aside(up_sums, 1), shift_aside(down_sums, -1))
    halves = [gram(total_rows, pair, kept, sent) for pair, sent in enumerate((up, down))]
    tiles = all_sum(mixed, 7, (halves[0][0],))
    rot = scaled(total_rows, 1, tiles, rotations, plan, (halves[1][0],))
    up, down, high, low = send_again(plan, kept, *moved, rot, halves[0][0])
    moved = shift(up, 1), shift(down, -1)
    result, halves_again = stay_again(total_rows, plan, high, low, rot, up, down)
    early, late = gram_sums(halves, halves_again)
    result, done = fill(result, *moved)
    return result, finish(early, late, done)


def solution(mesh):
    in_specs = (P("frame", "pair"), P(None, "pair", None, None), P(None, "pair", None))
    out_specs = (P("frame", "pair"), P(None, "frame", "pair", None))
    return jax.shard_map(local, mesh=mesh, in_specs=in_specs, out_specs=out_specs, check_vma=False)
```

```python
import functools

import jax
import jax.numpy as jnp
from jax import lax
from jax.experimental import pallas as pl
from jax.experimental.pallas import tpu as pltpu
from jax.sharding import PartitionSpec as P

BW = 256
STEPS = 2
READ = 256
CHUNK = 512
LONG = 512
VMEM = 16 * 1024 * 1024

epsilon = 1e-06

in_vmem = pl.BlockSpec(memory_space=pltpu.VMEM)
in_smem = pl.BlockSpec(memory_space=pltpu.SMEM)
in_hbm = pl.BlockSpec(memory_space=pltpu.HBM)
anywhere = pl.BlockSpec(memory_space=pl.ANY)


def f32(*shape):
    return jax.ShapeDtypeStruct(shape, jnp.float32)


def bf16(*shape):
    return jax.ShapeDtypeStruct(shape, jnp.bfloat16)


def params(limit=VMEM):
    return pltpu.CompilerParams(vmem_limit_bytes=limit)


def cost(flops, nbytes):
    return pl.CostEstimate(flops=flops, bytes_accessed=nbytes, transcendentals=0)


def split(x):
    high = x.astype(jnp.bfloat16)
    low = (x - high.astype(jnp.float32)).astype(jnp.bfloat16)
    return high, low


def add_squares(acc, slot, x):
    rows, cols = x.shape
    for half in range(cols // 128):
        piece = x[:, half * 128 : (half + 1) * 128]
        acc[2 * slot + half] += jnp.sum((piece * piece).reshape(rows // 8, 8, 128), axis=0)


def put_sums(sums_ref, acc):
    for row in range(8):
        sums_ref[row : row + 1, :] = jnp.sum(acc[row], axis=0, keepdims=True)


def first_kernel(x_ref, high_ref, low_ref, sums_ref, x, sem, acc):
    rows = x_ref.shape[0]
    copies = []
    for i in range(rows // READ):
        here = pl.ds(i * READ, READ)
        copies.append(pltpu.make_async_copy(x_ref.at[here, :], x.at[here, :], sem.at[i]))
    for copy in copies:
        copy.start()
    acc[...] = jnp.zeros_like(acc)
    for i, copy in enumerate(copies):
        here = slice(i * READ, (i + 1) * READ)
        copy.wait()
        for slot in range(4):
            piece = x[here, slot * BW : (slot + 1) * BW]
            add_squares(acc, slot, piece)
            high_ref[slot, here, :], low_ref[slot, here, :] = split(piece)
    put_sums(sums_ref, acc)


def first(columns):
    rows, cols = columns.shape
    return pl.pallas_call(
        first_kernel,
        in_specs=[in_hbm],
        out_specs=[in_vmem] * 3,
        out_shape=[bf16(4, rows, BW), bf16(4, rows, BW), f32(8, 128)],
        scratch_shapes=[
            pltpu.VMEM((rows, cols), jnp.float32),
            pltpu.SemaphoreType.DMA((rows // READ,)),
            pltpu.VMEM((8, 8, 128), jnp.float32),
        ],
        compiler_params=params(44 * 1024 * 1024),
        cost_estimate=cost(1 << 10, 1 << 10),
        name="first",
    )(columns)


def scale_kernel(total_rows, step, plan_ref, here_ref, there_ref, rot_ref, *refs):
    out_ref, scratch = refs[-2:]
    sums = here_ref[...] + there_ref[...]
    scratch[...] = jnp.sqrt(jnp.float32(total_rows)) * lax.rsqrt(sums + epsilon)
    for k in range(4):
        pair, half = k // 2, k % 2
        for part in range(2):
            row = scratch[pl.ds(2 * plan_ref[step, 0, k] + part, 1), :]
            column = jnp.broadcast_to(row, (128, 128)).T
            top = half * BW + part * 128
            for c in range(4):
                lanes = slice(c * 128, (c + 1) * 128)
                h, l = split(rot_ref[step, pair, top : top + 128, lanes] * column)
                out_ref[pair, top : top + 128, lanes] = h
                out_ref[pair, 2 * BW + top : 2 * BW + top + 128, lanes] = h
                out_ref[pair, 4 * BW + top : 4 * BW + top + 128, lanes] = l


def scaled(total_rows, step, sums, rotations, plan, after=()):
    return pl.pallas_call(
        functools.partial(scale_kernel, total_rows, step),
        in_specs=[in_smem] + [in_vmem] * 3 + [anywhere] * len(after),
        out_specs=in_vmem,
        out_shape=bf16(2, 6 * BW, 2 * BW),
        scratch_shapes=[pltpu.VMEM((8, 128), jnp.float32)],
        compiler_params=params(),
        cost_estimate=cost(1 << 10, 1 << 10),
        name="scale",
    )(plan, *sums, rotations, *after)


def pieces(rows, longest=CHUNK):
    count = -(-rows // longest)
    return [(k * (rows // count), rows // count) for k in range(count)]


def stacked(high_ref, low_ref, plan_ref, step, pair, row, count):
    slots = [plan_ref[step, 0, 2 * pair + k] for k in range(2)]
    h = [high_ref[slot, row : row + count, :] for slot in slots]
    l = [low_ref[slot, row : row + count, :] for slot in slots]
    return jnp.concatenate(h + l + h, axis=1)


def half_gram(nh, nl):
    turned = nh.T
    half = nh * jnp.bfloat16(0.5)
    top, bottom = turned[:BW], turned[BW:]
    dot = functools.partial(jnp.dot, preferred_element_type=jnp.float32)
    upper = jnp.concatenate([half[:, :BW], nh[:, BW:]], axis=1)
    above = dot(
        jnp.concatenate([top, top], axis=1), jnp.concatenate([upper, nl], axis=0)
    )
    below = jnp.concatenate(
        [
            dot(bottom, nl[:, :BW]),
            dot(
                jnp.concatenate([bottom, bottom], axis=1),
                jnp.concatenate([half[:, BW:], nl[:, BW:]], axis=0),
            ),
        ],
        axis=1,
    )
    return jnp.concatenate([above, below], axis=0)


def cut_gram(total_rows, pair, gram_acc, mine, other):
    half = gram_acc[pair]
    gram_acc[pair] = (half + half.T) * jnp.float32(1.0 / total_rows)
    x = lax.axis_index("frame") // 2
    near = x + 1 - 2 * (x % 2)
    blocks = (((x, 3 - x), (near, 3 - near)), ((x, near), (3 - x, 3 - near)))[pair]
    for ref, rows in zip((mine, other), blocks):
        for k in range(2):
            row = pl.multiple_of(128 * rows[k], 128)
            ref[k] = gram_acc[pair, pl.ds(row, 128), :]


def send_kernel(plan_ref, high_ref, low_ref, rot_ref, up, down, up_sums, down_sums, acc):
    acc[...] = jnp.zeros_like(acc)
    for r, count in pieces(up.shape[0]):
        for pair, sent in enumerate((up, down)):
            x = stacked(high_ref, low_ref, plan_ref, 0, pair, r, count)
            new = jnp.dot(x, rot_ref[pair, :, BW:], preferred_element_type=jnp.float32)
            sent[r : r + count, :] = new
            add_squares(acc, pair, new)
    for pair, sums in enumerate((up_sums, down_sums)):
        for half in range(2):
            sums[:, half * 128 : (half + 1) * 128] = acc[2 * pair + half]


def send(plan, high, low, rot):
    rows = high.shape[1]
    return pl.pallas_call(
        send_kernel,
        in_specs=[in_smem] + [in_vmem] * 3,
        out_specs=[in_vmem] * 4,
        out_shape=[f32(rows, BW)] * 2 + [f32(8, BW)] * 2,
        scratch_shapes=[pltpu.VMEM((4, 8, 128), jnp.float32)],
        compiler_params=params(),
        cost_estimate=cost(1 << 10, 1 << 10),
        name="send",
    )(plan, high, low, rot)


def stay_kernel(plan_ref, high_ref, low_ref, rot_ref, kept_high, kept_low, sums_ref, acc):
    acc[...] = jnp.zeros_like(acc)
    for r, count in pieces(high_ref.shape[1]):
        for pair in range(2):
            x = stacked(high_ref, low_ref, plan_ref, 0, pair, r, count)
            new = jnp.dot(x, rot_ref[pair, :, :BW], preferred_element_type=jnp.float32)
            h, l = split(new)
            kept_high[pair, r : r + count, :] = h
            kept_low[pair, r : r + count, :] = l
            add_squares(acc, pair, new)
    for row in range(4):
        sums_ref[row : row + 1, :] = jnp.sum(acc[row], axis=0, keepdims=True)
    sums_ref[4:8] = jnp.zeros((4, 128), jnp.float32)


def stay(plan, high, low, rot):
    rows = high.shape[1]
    *kept, sums = pl.pallas_call(
        stay_kernel,
        in_specs=[in_smem] + [in_vmem] * 3,
        out_specs=[in_vmem] * 3,
        out_shape=[bf16(2, rows, BW)] * 2 + [f32(8, 128)],
        scratch_shapes=[pltpu.VMEM((4, 8, 128), jnp.float32)],
        compiler_params=params(),
        cost_estimate=cost(1 << 10, 1 << 10),
        name="stay",
    )(plan, high, low, rot)
    return kept, sums


def gram_kernel(total_rows, pair, kept_high, kept_low, sent_ref, mine, other, gram_acc):
    for r, count in pieces(sent_ref.shape[0]):
        here = slice(r, r + count)
        h, l = split(sent_ref[here, :])
        gram = half_gram(
            jnp.concatenate([kept_high[pair, here, :], h], axis=1),
            jnp.concatenate([kept_low[pair, here, :], l], axis=1),
        )
        gram_acc[pair] = gram + gram_acc[pair] if r else gram
    cut_gram(total_rows, pair, gram_acc, mine, other)


def gram(total_rows, pair, kept, sent):
    return pl.pallas_call(
        functools.partial(gram_kernel, total_rows, pair),
        in_specs=[in_vmem] * 3,
        out_specs=[in_vmem] * 2,
        out_shape=[f32(2, 128, 2 * BW)] * 2,
        scratch_shapes=[pltpu.VMEM((2, 2 * BW, 2 * BW), jnp.float32)],
        compiler_params=params(),
        cost_estimate=cost(1 << 10, 1 << 10),
        name="gram",
    )(*kept, sent)


def send_again_kernel(plan_ref, kept_high, kept_low, up_in, down_in, rot_ref, _,
                      out_up, out_down, high_ref, low_ref):
    for slot in range(2):
        high_ref[slot] = kept_high[slot]
        low_ref[slot] = kept_low[slot]
    high_ref[2], low_ref[2] = split(up_in[...])
    high_ref[3], low_ref[3] = split(down_in[...])
    for r, count in pieces(up_in.shape[0]):
        for pair, sent in enumerate((out_up, out_down)):
            x = stacked(high_ref, low_ref, plan_ref, 1, pair, r, count)
            sent[r : r + count, :] = jnp.dot(
                x, rot_ref[pair, :, BW:], preferred_element_type=jnp.float32
            )


def send_again(plan, kept, up, down, rot, after):
    rows = up.shape[0]
    return pl.pallas_call(
        send_again_kernel,
        in_specs=[in_smem] + [in_vmem] * 5 + [anywhere],
        out_specs=[in_vmem] * 4,
        out_shape=[f32(rows, BW)] * 2 + [bf16(4, rows, BW)] * 2,
        compiler_params=params(),
        cost_estimate=cost(1 << 10, 1 << 10),
        name="send_again",
    )(plan, *kept, up, down, rot, after)


def stay_again_kernel(total_rows, plan_ref, high_ref, low_ref, rot_ref, up, down, result, *refs):
    outs, (gram_acc, kept_ref, sem) = refs[:4], refs[4:]
    copies = []
    for k, (r, count) in enumerate(pieces(up.shape[0], LONG)):
        here = slice(r, r + count)
        for pair, sent in enumerate((up, down)):
            x = stacked(high_ref, low_ref, plan_ref, 1, pair, r, count)
            new = jnp.dot(x, rot_ref[pair, :, :BW], preferred_element_type=jnp.float32)
            kept_ref[here, pair * BW : (pair + 1) * BW] = new
            h, l = split(new)
            sent_h, sent_l = split(sent[here, :])
            gram = half_gram(
                jnp.concatenate([h, sent_h], axis=1), jnp.concatenate([l, sent_l], axis=1)
            )
            gram_acc[pair] = gram + gram_acc[pair] if r else gram
        copies.append(
            pltpu.make_async_copy(
                kept_ref.at[pl.ds(r, count), :],
                result.at[pl.ds(r, count), pl.ds(0, 2 * BW)],
                sem.at[k],
            )
        )
        copies[-1].start()
    for pair in range(2):
        cut_gram(total_rows, pair, gram_acc, *outs[2 * pair : 2 * pair + 2])
    for copy in copies:
        copy.wait()


def stay_again(total_rows, plan, high, low, rot, up, down):
    rows = up.shape[0]
    result, *outs = pl.pallas_call(
        functools.partial(stay_again_kernel, total_rows),
        in_specs=[in_smem] + [in_vmem] * 5,
        out_specs=[in_hbm] + [in_vmem] * 4,
        out_shape=[f32(rows, 4 * BW)] + [f32(2, 128, 2 * BW)] * 4,
        scratch_shapes=[
            pltpu.VMEM((2, 2 * BW, 2 * BW), jnp.float32),
            pltpu.VMEM((rows, 2 * BW), jnp.float32),
            pltpu.SemaphoreType.DMA((len(pieces(rows, LONG)),)),
        ],
        compiler_params=params(),
        cost_estimate=cost(1 << 10, 1 << 10),
        name="stay_again",
    )(plan, high, low, rot, up, down)
    return result, (outs[:2], outs[2:])


def mix_kernel(own, before, after, out):
    out[0:4] = own[0:4]
    for k, ref in enumerate((before, after)):
        for half in range(2):
            row = 4 + 2 * k + half
            lanes = slice(half * 128, (half + 1) * 128)
            out[row : row + 1, :] = jnp.sum(ref[:, lanes], axis=0, keepdims=True)


def mix(own, before, after):
    return pl.pallas_call(
        mix_kernel,
        in_specs=[in_vmem] * 3,
        out_specs=in_vmem,
        out_shape=f32(8, 128),
        compiler_params=params(),
        cost_estimate=cost(1 << 10, 1 << 10),
        name="mix",
    )(own, before, after)


def add_kernel(mine, got, *refs):
    keep_ref, send_ref = refs[-2:]
    keep_ref[...] = mine[0] + got[0]
    send_ref[...] = mine[1] + got[1]


def add_first(mine, got, after):
    return pl.pallas_call(
        add_kernel,
        in_specs=[in_vmem] * 2 + [anywhere] * len(after),
        out_specs=[in_vmem] * 2,
        out_shape=[f32(mine.shape[1], 2 * BW)] * 2,
        compiler_params=params(),
        cost_estimate=cost(1 << 10, 1 << 10),
        name="add",
    )(mine, got, *after)


def halve_kernel(*refs):
    keep_ref, send_ref = refs[-2:]
    bit = lax.axis_index("frame") % 2
    for k in range(keep_ref.shape[0]):
        mine, got = refs[2 * k], refs[2 * k + 1]
        for ref, chosen in ((keep_ref, bit), (send_ref, 1 - bit)):
            rows = pl.ds(pl.multiple_of(64 * chosen, 64), 64)
            ref[k] = mine[rows, :] + got[rows, :]


def halve(terms):
    args = [array for term in terms for array in term]
    return pl.pallas_call(
        halve_kernel,
        in_specs=[in_vmem] * len(args),
        out_specs=[in_vmem] * 2,
        out_shape=[f32(len(terms), 64, 2 * BW)] * 2,
        compiler_params=params(),
        cost_estimate=cost(1 << 10, 1 << 10),
        name="halve",
    )(*args)


def begin_kernel(mine0, got0, mine1, got1, _, keep0, send0, keep1, send1):
    bit = lax.axis_index("frame") % 2
    for ref, chosen in ((keep0, bit), (send0, 1 - bit)):
        rows = pl.ds(pl.multiple_of(64 * chosen, 64), 64)
        ref[...] = mine0[:, rows, :] + got0[:, rows, :]
    keep1[...] = mine1[0] + got1[0]
    send1[...] = mine1[1] + got1[1]


def begin(args, after):
    return pl.pallas_call(
        begin_kernel,
        in_specs=[in_vmem] * 4 + [anywhere],
        out_specs=[in_vmem] * 4,
        out_shape=[f32(2, 64, 2 * BW)] * 2 + [f32(128, 2 * BW)] * 2,
        compiler_params=params(),
        cost_estimate=cost(1 << 10, 1 << 10),
        name="begin",
    )(*args, after)


def fill_kernel(_, up, down, out, done, sem):
    copies = [
        pltpu.make_async_copy(ref, out.at[:, pl.ds((2 + k) * BW, BW)], sem.at[k])
        for k, ref in enumerate((up, down))
    ]
    for copy in copies:
        copy.start()
    done[...] = jnp.zeros_like(done)
    for copy in copies:
        copy.wait()


def fill(out, up, down):
    return pl.pallas_call(
        fill_kernel,
        in_specs=[in_hbm, in_vmem, in_vmem],
        out_specs=[in_hbm, in_vmem],
        out_shape=[jax.ShapeDtypeStruct(out.shape, out.dtype), f32(8, 128)],
        input_output_aliases={0: 0},
        scratch_shapes=[pltpu.SemaphoreType.DMA((2,))],
        compiler_params=params(),
        cost_estimate=cost(1 << 10, 1 << 10),
        name="fill",
    )(out, up, down)


def finish_kernel(early_mine, early_got, mine, got, _, out):
    out[0, :, 0, :] = early_mine[...] + early_got[...]
    out[0, :, 1, :] = mine[2] + got[2]
    for pair in range(2):
        out[1, :, pair, :] = mine[pair] + got[pair]


def finish(early, late, after):
    return pl.pallas_call(
        finish_kernel,
        in_specs=[in_vmem] * 4 + [anywhere],
        out_specs=in_vmem,
        out_shape=f32(STEPS, 64, 2, 2 * BW),
        compiler_params=params(),
        cost_estimate=cost(1 << 10, 1 << 10),
        name="finish",
    )(*early, *late, after)


def shift(x, by):
    size = lax.axis_size("pair")
    return lax.ppermute(x, "pair", [(i, (i + by) % size) for i in range(size)])


def swap(x, bit):
    size = lax.axis_size("frame")
    return lax.ppermute(x, "frame", [(i, i ^ bit) for i in range(size)])


def shift_aside(x, by):
    frames, holders = lax.axis_size("frame"), lax.axis_size("pair")
    pairs = [
        (f * holders + h, (f ^ 2) * holders + (h + by) % holders)
        for f in range(frames)
        for h in range(holders)
    ]
    return lax.ppermute(x, ("frame", "pair"), pairs)


def add_kernel_of_four(a, b, c, d, *refs):
    refs[-1][...] = (a[...] + b[...]) + (c[...] + d[...])


def all_sum(x, across, after=()):
    x = pl.pallas_call(
        add_kernel_of_four,
        in_specs=[in_vmem] * 4 + [anywhere] * len(after),
        out_specs=in_vmem,
        out_shape=f32(8, 128),
        compiler_params=params(),
        cost_estimate=cost(1 << 10, 1 << 10),
        name="add_four",
    )(x, swap(x, 2), swap(x, 6), swap(x, 4), *after)
    return x, swap(x, across)


NEAR = ((2, 6), (6, 2))


def gram_sums(first_halves, last_halves):
    args = []
    for (mine, other), (here, _) in zip(first_halves, NEAR):
        args += [mine, swap(other, here)]
    mine, other, kept1, sent1 = begin(args, last_halves[0][0])
    kept, sent = add_first(mine, swap(other, 1), ())
    early = kept, swap(sent, NEAR[0][1])
    terms = []
    for (mine, other), (here, there) in zip(last_halves, NEAR):
        kept, sent = add_first(mine, swap(other, here), ())
        terms.append((kept, swap(sent, there)))
    terms.append((kept1, swap(sent1, NEAR[1][1])))
    mine, other = halve(terms)
    return early, (mine, swap(other, 1))


def local(columns, rotations, plan):
    total_rows = columns.shape[0] * lax.axis_size("frame")
    high, low, sums = first(columns)
    rot = scaled(total_rows, 0, all_sum(sums, 1), rotations, plan)
    up, down, up_sums, down_sums = send(plan, high, low, rot)
    moved = shift(up, 1), shift(down, -1)
    kept, own = stay(plan, high, low, rot)
    mixed = mix(own, shift_aside(up_sums, 1), shift_aside(down_sums, -1))
    halves = [gram(total_rows, pair, kept, sent) for pair, sent in enumerate((up, down))]
    tiles = all_sum(mixed, 3, (halves[0][0],))
    rot = scaled(total_rows, 1, tiles, rotations, plan, (halves[1][0],))
    up, down, high, low = send_again(plan, kept, *moved, rot, halves[0][0])
    moved = shift(up, 1), shift(down, -1)
    result, halves_again = stay_again(total_rows, plan, high, low, rot, up, down)
    early, late = gram_sums(halves, halves_again)
    result, done = fill(result, *moved)
    return result, finish(early, late, done)


def solution(mesh):
    in_specs = (P("frame", "pair"), P(None, "pair", None, None), P(None, "pair", None))
    out_specs = (P("frame", "pair"), P(None, "frame", "pair", None))
    return jax.shard_map(local, mesh=mesh, in_specs=in_specs, out_specs=out_specs, check_vma=False)
```

```python
import functools

import jax
import jax.numpy as jnp
from jax import lax
from jax.experimental import pallas as pl
from jax.experimental.pallas import tpu as pltpu
from jax.sharding import PartitionSpec as P

BW = 256
STEPS = 2
READ = 256
CHUNK = 512
LONG = 512
VMEM = 16 * 1024 * 1024

epsilon = 1e-06

in_vmem = pl.BlockSpec(memory_space=pltpu.VMEM)
in_smem = pl.BlockSpec(memory_space=pltpu.SMEM)
in_hbm = pl.BlockSpec(memory_space=pltpu.HBM)
anywhere = pl.BlockSpec(memory_space=pl.ANY)


def f32(*shape):
    return jax.ShapeDtypeStruct(shape, jnp.float32)


def bf16(*shape):
    return jax.ShapeDtypeStruct(shape, jnp.bfloat16)


def params(limit=VMEM):
    return pltpu.CompilerParams(vmem_limit_bytes=limit)


def cost(flops, nbytes):
    return pl.CostEstimate(flops=flops, bytes_accessed=nbytes, transcendentals=0)


def split(x):
    high = x.astype(jnp.bfloat16)
    low = (x - high.astype(jnp.float32)).astype(jnp.bfloat16)
    return high, low


def add_squares(acc, slot, x):
    rows, cols = x.shape
    for half in range(cols // 128):
        piece = x[:, half * 128 : (half + 1) * 128]
        acc[2 * slot + half] += jnp.sum((piece * piece).reshape(rows // 8, 8, 128), axis=0)


def put_sums(sums_ref, acc):
    for row in range(8):
        sums_ref[row : row + 1, :] = jnp.sum(acc[row], axis=0, keepdims=True)


def first_kernel(x_ref, high_ref, low_ref, sums_ref, x, sem, acc):
    rows = x_ref.shape[0]
    copies = []
    for i in range(rows // READ):
        here = pl.ds(i * READ, READ)
        copies.append(pltpu.make_async_copy(x_ref.at[here, :], x.at[here, :], sem.at[i]))
    for copy in copies:
        copy.start()
    acc[...] = jnp.zeros_like(acc)
    for i, copy in enumerate(copies):
        here = slice(i * READ, (i + 1) * READ)
        copy.wait()
        for slot in range(4):
            piece = x[here, slot * BW : (slot + 1) * BW]
            add_squares(acc, slot, piece)
            high_ref[slot, here, :], low_ref[slot, here, :] = split(piece)
    put_sums(sums_ref, acc)


def first(columns):
    rows, cols = columns.shape
    return pl.pallas_call(
        first_kernel,
        in_specs=[in_hbm],
        out_specs=[in_vmem] * 3,
        out_shape=[bf16(4, rows, BW), bf16(4, rows, BW), f32(8, 128)],
        scratch_shapes=[
            pltpu.VMEM((rows, cols), jnp.float32),
            pltpu.SemaphoreType.DMA((rows // READ,)),
            pltpu.VMEM((8, 8, 128), jnp.float32),
        ],
        compiler_params=params(44 * 1024 * 1024),
        cost_estimate=cost(1 << 10, 1 << 10),
        name="first",
    )(columns)


def scale_kernel(total_rows, step, plan_ref, here_ref, there_ref, rot_ref, *refs):
    out_ref, scratch = refs[-2:]
    sums = here_ref[...] + there_ref[...]
    scratch[...] = jnp.sqrt(jnp.float32(total_rows)) * lax.rsqrt(sums + epsilon)
    for k in range(4):
        pair, half = k // 2, k % 2
        for part in range(2):
            row = scratch[pl.ds(2 * plan_ref[step, 0, k] + part, 1), :]
            column = jnp.broadcast_to(row, (128, 128)).T
            top = half * BW + part * 128
            for c in range(4):
                lanes = slice(c * 128, (c + 1) * 128)
                h, l = split(rot_ref[step, pair, top : top + 128, lanes] * column)
                out_ref[pair, top : top + 128, lanes] = h
                out_ref[pair, 2 * BW + top : 2 * BW + top + 128, lanes] = h
                out_ref[pair, 4 * BW + top : 4 * BW + top + 128, lanes] = l


def scaled(total_rows, step, sums, rotations, plan, after=()):
    return pl.pallas_call(
        functools.partial(scale_kernel, total_rows, step),
        in_specs=[in_smem] + [in_vmem] * 3 + [anywhere] * len(after),
        out_specs=in_vmem,
        out_shape=bf16(2, 6 * BW, 2 * BW),
        scratch_shapes=[pltpu.VMEM((8, 128), jnp.float32)],
        compiler_params=params(),
        cost_estimate=cost(1 << 10, 1 << 10),
        name="scale",
    )(plan, *sums, rotations, *after)


def pieces(rows, longest=CHUNK):
    count = -(-rows // longest)
    return [(k * (rows // count), rows // count) for k in range(count)]


def stacked(high_ref, low_ref, plan_ref, step, pair, row, count):
    slots = [plan_ref[step, 0, 2 * pair + k] for k in range(2)]
    h = [high_ref[slot, row : row + count, :] for slot in slots]
    l = [low_ref[slot, row : row + count, :] for slot in slots]
    return jnp.concatenate(h + l + h, axis=1)


def half_gram(nh, nl):
    turned = nh.T
    half = nh * jnp.bfloat16(0.5)
    top, bottom = turned[:BW], turned[BW:]
    dot = functools.partial(jnp.dot, preferred_element_type=jnp.float32)
    upper = jnp.concatenate([half[:, :BW], nh[:, BW:]], axis=1)
    above = dot(
        jnp.concatenate([top, top], axis=1), jnp.concatenate([upper, nl], axis=0)
    )
    below = jnp.concatenate(
        [
            dot(bottom, nl[:, :BW]),
            dot(
                jnp.concatenate([bottom, bottom], axis=1),
                jnp.concatenate([half[:, BW:], nl[:, BW:]], axis=0),
            ),
        ],
        axis=1,
    )
    return jnp.concatenate([above, below], axis=0)


def cut_gram(total_rows, pair, gram_acc, mine, other):
    half = gram_acc[pair]
    gram_acc[pair] = (half + half.T) * jnp.float32(1.0 / total_rows)
    x = lax.axis_index("frame") // 2
    near = x + 1 - 2 * (x % 2)
    blocks = (((x, near), (3 - x, 3 - near)), ((x, 3 - x), (near, 3 - near)))[pair]
    for ref, rows in zip((mine, other), blocks):
        for k in range(2):
            row = pl.multiple_of(128 * rows[k], 128)
            ref[k] = gram_acc[pair, pl.ds(row, 128), :]


def send_kernel(plan_ref, high_ref, low_ref, rot_ref, up, down, up_sums, down_sums, acc):
    acc[...] = jnp.zeros_like(acc)
    for r, count in pieces(up.shape[0]):
        for pair, sent in enumerate((up, down)):
            x = stacked(high_ref, low_ref, plan_ref, 0, pair, r, count)
            new = jnp.dot(x, rot_ref[pair, :, BW:], preferred_element_type=jnp.float32)
            sent[r : r + count, :] = new
            add_squares(acc, pair, new)
    for pair, sums in enumerate((up_sums, down_sums)):
        for half in range(2):
            sums[:, half * 128 : (half + 1) * 128] = acc[2 * pair + half]


def send(plan, high, low, rot):
    rows = high.shape[1]
    return pl.pallas_call(
        send_kernel,
        in_specs=[in_smem] + [in_vmem] * 3,
        out_specs=[in_vmem] * 4,
        out_shape=[f32(rows, BW)] * 2 + [f32(8, BW)] * 2,
        scratch_shapes=[pltpu.VMEM((4, 8, 128), jnp.float32)],
        compiler_params=params(),
        cost_estimate=cost(1 << 10, 1 << 10),
        name="send",
    )(plan, high, low, rot)


def stay_kernel(plan_ref, high_ref, low_ref, rot_ref, kept_high, kept_low, sums_ref, acc):
    acc[...] = jnp.zeros_like(acc)
    for r, count in pieces(high_ref.shape[1]):
        for pair in range(2):
            x = stacked(high_ref, low_ref, plan_ref, 0, pair, r, count)
            new = jnp.dot(x, rot_ref[pair, :, :BW], preferred_element_type=jnp.float32)
            h, l = split(new)
            kept_high[pair, r : r + count, :] = h
            kept_low[pair, r : r + count, :] = l
            add_squares(acc, pair, new)
    for row in range(4):
        sums_ref[row : row + 1, :] = jnp.sum(acc[row], axis=0, keepdims=True)
    sums_ref[4:8] = jnp.zeros((4, 128), jnp.float32)


def stay(plan, high, low, rot):
    rows = high.shape[1]
    *kept, sums = pl.pallas_call(
        stay_kernel,
        in_specs=[in_smem] + [in_vmem] * 3,
        out_specs=[in_vmem] * 3,
        out_shape=[bf16(2, rows, BW)] * 2 + [f32(8, 128)],
        scratch_shapes=[pltpu.VMEM((4, 8, 128), jnp.float32)],
        compiler_params=params(),
        cost_estimate=cost(1 << 10, 1 << 10),
        name="stay",
    )(plan, high, low, rot)
    return kept, sums


def gram_kernel(total_rows, pair, kept_high, kept_low, sent_ref, mine, other, gram_acc):
    for r, count in pieces(sent_ref.shape[0]):
        here = slice(r, r + count)
        h, l = split(sent_ref[here, :])
        gram = half_gram(
            jnp.concatenate([kept_high[pair, here, :], h], axis=1),
            jnp.concatenate([kept_low[pair, here, :], l], axis=1),
        )
        gram_acc[pair] = gram + gram_acc[pair] if r else gram
    cut_gram(total_rows, pair, gram_acc, mine, other)


def gram(total_rows, pair, kept, sent):
    return pl.pallas_call(
        functools.partial(gram_kernel, total_rows, pair),
        in_specs=[in_vmem] * 3,
        out_specs=[in_vmem] * 2,
        out_shape=[f32(2, 128, 2 * BW)] * 2,
        scratch_shapes=[pltpu.VMEM((2, 2 * BW, 2 * BW), jnp.float32)],
        compiler_params=params(),
        cost_estimate=cost(1 << 10, 1 << 10),
        name="gram",
    )(*kept, sent)


def send_again_kernel(plan_ref, kept_high, kept_low, up_in, down_in, rot_ref, _,
                      out_up, out_down, high_ref, low_ref):
    for slot in range(2):
        high_ref[slot] = kept_high[slot]
        low_ref[slot] = kept_low[slot]
    high_ref[2], low_ref[2] = split(up_in[...])
    high_ref[3], low_ref[3] = split(down_in[...])
    for r, count in pieces(up_in.shape[0]):
        for pair, sent in enumerate((out_up, out_down)):
            x = stacked(high_ref, low_ref, plan_ref, 1, pair, r, count)
            sent[r : r + count, :] = jnp.dot(
                x, rot_ref[pair, :, BW:], preferred_element_type=jnp.float32
            )


def send_again(plan, kept, up, down, rot, after):
    rows = up.shape[0]
    return pl.pallas_call(
        send_again_kernel,
        in_specs=[in_smem] + [in_vmem] * 5 + [anywhere],
        out_specs=[in_vmem] * 4,
        out_shape=[f32(rows, BW)] * 2 + [bf16(4, rows, BW)] * 2,
        compiler_params=params(),
        cost_estimate=cost(1 << 10, 1 << 10),
        name="send_again",
    )(plan, *kept, up, down, rot, after)


def stay_again_kernel(total_rows, plan_ref, high_ref, low_ref, rot_ref, up, down, result, *refs):
    outs, (gram_acc, kept_ref, sem) = refs[:4], refs[4:]
    copies = []
    for k, (r, count) in enumerate(pieces(up.shape[0], LONG)):
        here = slice(r, r + count)
        for pair, sent in enumerate((up, down)):
            x = stacked(high_ref, low_ref, plan_ref, 1, pair, r, count)
            new = jnp.dot(x, rot_ref[pair, :, :BW], preferred_element_type=jnp.float32)
            kept_ref[here, pair * BW : (pair + 1) * BW] = new
            h, l = split(new)
            sent_h, sent_l = split(sent[here, :])
            gram = half_gram(
                jnp.concatenate([h, sent_h], axis=1), jnp.concatenate([l, sent_l], axis=1)
            )
            gram_acc[pair] = gram + gram_acc[pair] if r else gram
        copies.append(
            pltpu.make_async_copy(
                kept_ref.at[pl.ds(r, count), :],
                result.at[pl.ds(r, count), pl.ds(0, 2 * BW)],
                sem.at[k],
            )
        )
        copies[-1].start()
    for pair in range(2):
        cut_gram(total_rows, pair, gram_acc, *outs[2 * pair : 2 * pair + 2])
    for copy in copies:
        copy.wait()


def stay_again(total_rows, plan, high, low, rot, up, down):
    rows = up.shape[0]
    result, *outs = pl.pallas_call(
        functools.partial(stay_again_kernel, total_rows),
        in_specs=[in_smem] + [in_vmem] * 5,
        out_specs=[in_hbm] + [in_vmem] * 4,
        out_shape=[f32(rows, 4 * BW)] + [f32(2, 128, 2 * BW)] * 4,
        scratch_shapes=[
            pltpu.VMEM((2, 2 * BW, 2 * BW), jnp.float32),
            pltpu.VMEM((rows, 2 * BW), jnp.float32),
            pltpu.SemaphoreType.DMA((len(pieces(rows, LONG)),)),
        ],
        compiler_params=params(),
        cost_estimate=cost(1 << 10, 1 << 10),
        name="stay_again",
    )(plan, high, low, rot, up, down)
    return result, (outs[:2], outs[2:])


def mix_kernel(own, before, after, out):
    out[0:4] = own[0:4]
    for k, ref in enumerate((before, after)):
        for half in range(2):
            row = 4 + 2 * k + half
            lanes = slice(half * 128, (half + 1) * 128)
            out[row : row + 1, :] = jnp.sum(ref[:, lanes], axis=0, keepdims=True)


def mix(own, before, after):
    return pl.pallas_call(
        mix_kernel,
        in_specs=[in_vmem] * 3,
        out_specs=in_vmem,
        out_shape=f32(8, 128),
        compiler_params=params(),
        cost_estimate=cost(1 << 10, 1 << 10),
        name="mix",
    )(own, before, after)


def add_kernel(mine, got, *refs):
    keep_ref, send_ref = refs[-2:]
    keep_ref[...] = mine[0] + got[0]
    send_ref[...] = mine[1] + got[1]


def add_first(mine, got, after):
    return pl.pallas_call(
        add_kernel,
        in_specs=[in_vmem] * 2 + [anywhere] * len(after),
        out_specs=[in_vmem] * 2,
        out_shape=[f32(mine.shape[1], 2 * BW)] * 2,
        compiler_params=params(),
        cost_estimate=cost(1 << 10, 1 << 10),
        name="add",
    )(mine, got, *after)


def halve_kernel(*refs):
    keep_ref, send_ref = refs[-2:]
    bit = lax.axis_index("frame") % 2
    for k in range(keep_ref.shape[0]):
        mine, got = refs[2 * k], refs[2 * k + 1]
        for ref, chosen in ((keep_ref, bit), (send_ref, 1 - bit)):
            rows = pl.ds(pl.multiple_of(64 * chosen, 64), 64)
            ref[k] = mine[rows, :] + got[rows, :]


def halve(terms):
    args = [array for term in terms for array in term]
    return pl.pallas_call(
        halve_kernel,
        in_specs=[in_vmem] * len(args),
        out_specs=[in_vmem] * 2,
        out_shape=[f32(len(terms), 64, 2 * BW)] * 2,
        compiler_params=params(),
        cost_estimate=cost(1 << 10, 1 << 10),
        name="halve",
    )(*args)


def begin_kernel(mine0, got0, mine1, got1, _, keep0, send0, keep1, send1):
    bit = lax.axis_index("frame") % 2
    for ref, chosen in ((keep0, bit), (send0, 1 - bit)):
        rows = pl.ds(pl.multiple_of(64 * chosen, 64), 64)
        ref[...] = mine0[:, rows, :] + got0[:, rows, :]
    keep1[...] = mine1[0] + got1[0]
    send1[...] = mine1[1] + got1[1]


def begin(args, after):
    return pl.pallas_call(
        begin_kernel,
        in_specs=[in_vmem] * 4 + [anywhere],
        out_specs=[in_vmem] * 4,
        out_shape=[f32(2, 64, 2 * BW)] * 2 + [f32(128, 2 * BW)] * 2,
        compiler_params=params(),
        cost_estimate=cost(1 << 10, 1 << 10),
        name="begin",
    )(*args, after)


def fill_kernel(_, up, down, out, done, sem):
    copies = [
        pltpu.make_async_copy(ref, out.at[:, pl.ds((2 + k) * BW, BW)], sem.at[k])
        for k, ref in enumerate((up, down))
    ]
    for copy in copies:
        copy.start()
    done[...] = jnp.zeros_like(done)
    for copy in copies:
        copy.wait()


def fill(out, up, down):
    return pl.pallas_call(
        fill_kernel,
        in_specs=[in_hbm, in_vmem, in_vmem],
        out_specs=[in_hbm, in_vmem],
        out_shape=[jax.ShapeDtypeStruct(out.shape, out.dtype), f32(8, 128)],
        input_output_aliases={0: 0},
        scratch_shapes=[pltpu.SemaphoreType.DMA((2,))],
        compiler_params=params(),
        cost_estimate=cost(1 << 10, 1 << 10),
        name="fill",
    )(out, up, down)


def finish_kernel(early_mine, early_got, mine, got, _, out):
    out[0, :, 0, :] = early_mine[...] + early_got[...]
    out[0, :, 1, :] = mine[2] + got[2]
    for pair in range(2):
        out[1, :, pair, :] = mine[pair] + got[pair]


def finish(early, late, after):
    return pl.pallas_call(
        finish_kernel,
        in_specs=[in_vmem] * 4 + [anywhere],
        out_specs=in_vmem,
        out_shape=f32(STEPS, 64, 2, 2 * BW),
        compiler_params=params(),
        cost_estimate=cost(1 << 10, 1 << 10),
        name="finish",
    )(*early, *late, after)


def shift(x, by):
    size = lax.axis_size("pair")
    return lax.ppermute(x, "pair", [(i, (i + by) % size) for i in range(size)])


def swap(x, bit):
    size = lax.axis_size("frame")
    return lax.ppermute(x, "frame", [(i, i ^ bit) for i in range(size)])


def shift_aside(x, by):
    frames, holders = lax.axis_size("frame"), lax.axis_size("pair")
    pairs = [
        (f * holders + h, (f ^ 2) * holders + (h + by) % holders)
        for f in range(frames)
        for h in range(holders)
    ]
    return lax.ppermute(x, ("frame", "pair"), pairs)


def add_kernel_of_four(a, b, c, d, *refs):
    refs[-1][...] = (a[...] + b[...]) + (c[...] + d[...])


def all_sum(x, across, after=()):
    x = pl.pallas_call(
        add_kernel_of_four,
        in_specs=[in_vmem] * 4 + [anywhere] * len(after),
        out_specs=in_vmem,
        out_shape=f32(8, 128),
        compiler_params=params(),
        cost_estimate=cost(1 << 10, 1 << 10),
        name="add_four",
    )(x, swap(x, 2), swap(x, 6), swap(x, 4), *after)
    return x, swap(x, across)


NEAR = ((6, 2), (2, 6))


def gram_sums(first_halves, last_halves):
    args = []
    for (mine, other), (here, _) in zip(first_halves, NEAR):
        args += [mine, swap(other, here)]
    mine, other, kept1, sent1 = begin(args, last_halves[0][0])
    kept, sent = add_first(mine, swap(other, 1), ())
    early = kept, swap(sent, NEAR[0][1])
    terms = []
    for (mine, other), (here, there) in zip(last_halves, NEAR):
        kept, sent = add_first(mine, swap(other, here), ())
        terms.append((kept, swap(sent, there)))
    terms.append((kept1, swap(sent1, NEAR[1][1])))
    mine, other = halve(terms)
    return early, (mine, swap(other, 1))


def local(columns, rotations, plan):
    total_rows = columns.shape[0] * lax.axis_size("frame")
    high, low, sums = first(columns)
    rot = scaled(total_rows, 0, all_sum(sums, 1), rotations, plan)
    up, down, up_sums, down_sums = send(plan, high, low, rot)
    moved = shift(up, 1), shift(down, -1)
    kept, own = stay(plan, high, low, rot)
    mixed = mix(own, shift_aside(up_sums, 1), shift_aside(down_sums, -1))
    halves = [gram(total_rows, pair, kept, sent) for pair, sent in enumerate((up, down))]
    tiles = all_sum(mixed, 3, (halves[0][0],))
    rot = scaled(total_rows, 1, tiles, rotations, plan, (halves[1][0],))
    up, down, high, low = send_again(plan, kept, *moved, rot, halves[0][0])
    moved = shift(up, 1), shift(down, -1)
    result, halves_again = stay_again(total_rows, plan, high, low, rot, up, down)
    early, late = gram_sums(halves, halves_again)
    result, done = fill(result, *moved)
    return result, finish(early, late, done)


def solution(mesh):
    in_specs = (P("frame", "pair"), P(None, "pair", None, None), P(None, "pair", None))
    out_specs = (P("frame", "pair"), P(None, "frame", "pair", None))
    return jax.shard_map(local, mesh=mesh, in_specs=in_specs, out_specs=out_specs, check_vma=False)
```
